32 devices in a mesh: ctx: 4 (over y, x), ch: 8 (over z, core).
Axes of the slice: x: 2, y: 2, z: 4, core: 2. Of those that a mesh axis runs over, the one named last changes fastest.
Arguments:
- streams: bfloat16 [16384, 3, 2048], P(('ctx', 'ch')), may hold values from -6 to 6
- load_counts: int32 [4, 8], P('ctx'), may hold values from 1 to 512, 2048 in all within a row
- seg_ids: int32 [8192], P('ctx'), may hold values from 0 to 3, never falling along the last dimension, each value on 1 to 4096 neighbouring positions
- rates: float32 [2048, 16], P('ch'), may hold values from 1.2207031e-05 to 0.05
- residues: float32 [2048, 16], P('ch'), may hold values from -1.5 to 1.5
- skip: float32 [2048], P('ch'), may hold values from 0.5 to 1.5
Outputs:
- mixed: bfloat16 [8192, 2048], P('ctx', 'ch')
The draws below stay inside these ranges and needn't reach their ends.
Inputs may be any that keep to these rules, and one draw needn't show every extreme that they name: `load_counts`: each row sums to 2048 and its largest entry equals 512. `seg_ids`: never falls; each segment holds 1 to 4096 positions, one exactly that many.
All inputs are finite; a program needn't handle non-finite values.
Results may differ from the reference program's by a relative error of at most 0.0049.
Values may be sent and summed in bfloat16 or wider, within the bound.
A program may use at most 192 MiB of HBM per device.

```python
import math
import jax
import jax.numpy as jnp
import numpy as np
from jax import lax

ORDER = 16
L_DEV = 2048
SEGS = 4
D = 2048
SEQ = 8192
LOAD_CAP = 512
N_CTX = 4
N_CH = 8


def draw_rates(key, part):
    key_slow, key_level = jax.random.split(key, 2)
    slow = jax.random.bernoulli(key_slow, 0.5, (D, ORDER))
    level = jax.random.uniform(key_level, (D, ORDER), jnp.float32)
    low_rate = 0.1 / SEQ
    mid_rate = 1.0 / SEQ
    slow_rate = low_rate * (mid_rate / low_rate) ** level
    fast_rate = mid_rate * (0.05 / mid_rate) ** level
    return jnp.where(slow, slow_rate, fast_rate).astype(jnp.float32)


def levels(rng, shape, cuts, smallest, high):
    factor_of = 1.0
    for dim, blocks in cuts:
        draws = jax.random.uniform(jax.random.fold_in(jax.random.fold_in(rng, 6), dim), (blocks,), jnp.float32, smallest / len(cuts), high / len(cuts))
        factor_of = factor_of * jnp.repeat(jnp.exp(draws), shape[dim] // blocks).reshape((-1,) + (1,) * (len(shape) - 1 - dim))
    return factor_of


def split_up(count, total, bound, skew):
    portions = [(1 << 20) // math.isqrt(rank ** skew) + 1 for rank in range(2, count + 1)]
    surplus, given = total - bound - (count - 1), [1] * (count - 1)
    while surplus > 0:
        movable = [i for i in range(count - 1) if given[i] < bound]
        mass, left = sum([portions[i] for i in movable]), surplus
        for i in movable:
            extra = min(bound - given[i], max(1, left * portions[i] // mass), surplus)
            given[i] = given[i] + extra
            surplus = surplus - extra
    return np.array([bound] + given)


def ragged(key, number_of, total, reach, skew):
    if number_of == 2:
        one = jax.random.randint(key, (), max(1, total - reach), min(reach, total - 1) + 1)
        return jnp.stack([one, total - one])
    tallies = jnp.asarray(split_up(number_of, total, reach, skew), jnp.int32)
    twos = (number_of - 1) // 2
    giver, sink = tallies[1:1 + 2 * twos:2], tallies[2:2 + 2 * twos:2]
    slack = jnp.minimum(giver - 1, reach - sink)
    moved = jax.random.randint(jax.random.fold_in(key, 1), (twos,), 0, 1 << 20) % (slack + 1)
    tallies = tallies.at[1:1 + 2 * twos:2].set(giver - moved).at[2:2 + 2 * twos:2].set(sink + moved)
    return tallies[jax.random.permutation(jax.random.fold_in(key, 2), number_of)]


def bell_draw(own_key, extent, scale, most, cuts=(), held_as=jnp.bfloat16):
    level = levels(own_key, extent, cuts, -0.22, 0.18) if cuts else 1.0
    values = jax.random.normal(own_key, extent, jnp.float32) * scale * level
    return jnp.minimum(jnp.maximum(values, -most), most).astype(held_as)


def setup_inputs(seed: int = 0) -> dict:
    key_list = jax.random.split(jax.random.key(seed), 7)
    return {
        "streams": bell_draw(key_list[0], (N_CTX * N_CH * LOAD_CAP, 3, D), 1.0, 6.0, ((0, 32),)),
        "load_counts": jax.vmap(lambda own: ragged(own, N_CH, L_DEV, LOAD_CAP, 2))(jax.random.split(key_list[1], N_CTX)).reshape((N_CTX, N_CH)).astype(jnp.int32),
        "seg_ids": jnp.searchsorted(jnp.cumsum(ragged(key_list[2], SEGS, SEQ, SEQ // 2, 1)), jnp.arange(SEQ), side="right").astype(jnp.int32),
        "rates": draw_rates(jax.random.fold_in(key_list[6], 71), 0),
        "residues": bell_draw(key_list[4], (D, ORDER), ORDER ** -0.5, 1.5, ((0, 8),), jnp.float32),
        "skip": jnp.clip(0.5 + 1.0 * jax.random.uniform(key_list[5], (D,), jnp.float32) ** levels(key_list[5], (D,), ((0, 8),), -0.2, 0.2), 0.5, 1.5),
    }


def reference(streams, load_counts, seg_ids, rates, residues, skip):
    loaded = streams.reshape(N_CTX, N_CH, LOAD_CAP, 3, D)
    position = jnp.arange(L_DEV, dtype=jnp.int32)
    ending = jnp.cumsum(load_counts, axis=1).astype(jnp.int32)
    passed = ending[:, None, :] <= position[None, :, None]
    source = lax.optimization_barrier(jnp.sum(passed.astype(jnp.int32), axis=2)).astype(jnp.int32)
    starts = lax.optimization_barrier(jnp.sum(jnp.where(passed, load_counts[:, None, :], 0), axis=2)).astype(jnp.int32)
    slot_index = (position[None, :] - starts).astype(jnp.int32)
    span_ids = jnp.broadcast_to(jnp.arange(N_CTX, dtype=jnp.int32)[:, None], (N_CTX, L_DEV))
    placed = loaded[span_ids, source, slot_index].reshape(SEQ, 3, D)
    query = placed[:, 0]
    signal = (placed[:, 1].astype(jnp.float32) * placed[:, 2].astype(jnp.float32)).astype(jnp.bfloat16)
    decay = jnp.exp(-rates)
    gain = jnp.sqrt(-jnp.expm1(-2.0 * rates))
    keep = jnp.concatenate([jnp.zeros((1,), jnp.float32), (seg_ids[1:] == seg_ids[:-1]).astype(jnp.float32)])

    def advance(state, inputs):
        signal_row, keep_row = inputs
        state = keep_row * decay * state + gain * signal_row[:, None]
        return (state, lax.optimization_barrier(jnp.sum(residues * state, axis=1)))
    _, conv = lax.scan(advance, jnp.zeros((D, ORDER), jnp.float32), (signal.astype(jnp.float32), keep))
    mixed = query.astype(jnp.float32) * (conv + skip[None, :] * signal.astype(jnp.float32))
    return mixed.astype(jnp.bfloat16)
```

```python
import functools

import jax
import jax.numpy as jnp
from jax import lax
from jax.experimental import pallas as pl
from jax.experimental.pallas import tpu as pltpu
from jax.sharding import PartitionSpec as P

LANES = 128
GROUP = 8
TILE = 64
F32 = jnp.float32
BF16 = jnp.bfloat16


def product(k, v):
    return (k.astype(F32) * v.astype(F32)).astype(BF16).astype(F32)


def end_state_kernel(modes, count_ref, keep_ref, slow_ref, k_ref, v_ref, decay_ref, state_ref):
    block = pl.program_id(0)
    rows = k_ref.shape[2]
    count = count_ref[0]

    @pl.when(block == 0)
    def _():
        state_ref[...] = jnp.zeros_like(state_ref)

    def group(r, slow):
        at = pl.ds(r, GROUP)
        x = product(k_ref[0, at], v_ref[0, at])
        first = block * TILE + r
        for h in range(0, rows, 8):
            s = [state_ref[n, h:h + 8] for n in range(modes)]
            d = [decay_ref[n, h:h + 8] for n in range(modes)]
            for t in range(GROUP):
                xt = x[t, h:h + 8]
                if slow:
                    kept = keep_ref[first + t]
                    inside = first + t < count
                    s = [jnp.where(inside, s[n] * (d[n] * kept) + xt, s[n]) for n in range(modes)]
                else:
                    s = [s[n] * d[n] + xt for n in range(modes)]
            for n in range(modes):
                state_ref[n, h:h + 8] = s[n]

    def step(g, carry):
        r = pl.multiple_of(g * GROUP, GROUP)
        is_slow = slow_ref[block * (TILE // GROUP) + g] != 0

        @pl.when(is_slow)
        def _():
            group(r, True)

        @pl.when(jnp.logical_not(is_slow))
        def _():
            group(r, False)

        return carry

    todo = jnp.clip((count - block * TILE + GROUP - 1) // GROUP, 0, TILE // GROUP)
    lax.fori_loop(0, todo, step, 0)


def mix_kernel(modes, count_ref, keep_ref, slow_ref, q_ref, k_ref, v_ref, decay_ref, weight_ref, skip_ref, init_ref, out_ref, state_ref):
    block = pl.program_id(0)
    rows = k_ref.shape[2]
    count = count_ref[0]

    @pl.when(block == 0)
    def _():
        state_ref[...] = init_ref[...]

    def group(r, slow):
        at = pl.ds(r, GROUP)
        x = product(k_ref[0, at], v_ref[0, at])
        q = q_ref[0, at].astype(F32)
        first = block * TILE + r
        parts = []
        for h in range(0, rows, 8):
            s = [state_ref[n, h:h + 8] for n in range(modes)]
            d = [decay_ref[n, h:h + 8] for n in range(modes)]
            w = [weight_ref[n, h:h + 8] for n in range(modes)]
            skip = skip_ref[h:h + 8]
            mixed = []
            for t in range(GROUP):
                xt = x[t, h:h + 8]
                if slow:
                    kept = keep_ref[first + t]
                    s = [s[n] * (d[n] * kept) + xt for n in range(modes)]
                else:
                    s = [s[n] * d[n] + xt for n in range(modes)]
                terms = [s[n] * w[n] for n in range(modes)]
                while len(terms) > 1:
                    terms = [a + b for a, b in zip(terms[::2], terms[1::2])]
                mixed.append(q[t, h:h + 8] * (terms[0] + skip * xt))
            for n in range(modes):
                state_ref[n, h:h + 8] = s[n]
            parts.append(mixed)
        for t in range(GROUP):
            whole = jnp.concatenate([part[t] for part in parts], axis=0).astype(BF16)
            for g in range(rows // 2):
                out_ref[g, r + t] = whole[2 * g:2 * g + 2]

    def step(g, carry):
        r = pl.multiple_of(g * GROUP, GROUP)
        is_slow = slow_ref[block * (TILE // GROUP) + g] != 0

        @pl.when(is_slow)
        def _():
            group(r, True)

        @pl.when(jnp.logical_not(is_slow))
        def _():
            group(r, False)

        return carry

    todo = jnp.clip((count - block * TILE + GROUP - 1) // GROUP, 0, TILE // GROUP)
    lax.fori_loop(0, todo, step, 0)


def pack_kernel(bits, counts_ref, starts_ref, in_ref, out_ref, sems):
    shards_n = in_ref.shape[0]

    def copies(j, b, act):
        count = counts_ref[j]
        size = 1 << b
        offset = (count >> (b + 1)) << (b + 1)

        @pl.when((count >> b) & 1 == 1)
        def _():
            copy = pltpu.make_async_copy(
                in_ref.at[j, pl.ds(offset, size)],
                out_ref.at[pl.ds(starts_ref[j] + offset, size)],
                sems.at[j, b],
            )
            if act:
                copy.start()
            else:
                copy.wait()

    def begin(j, carry):
        for b in range(bits):
            copies(j, b, True)
        return carry

    def finish(j, carry):
        for b in range(bits):
            copies(j, b, False)
        return carry

    lax.fori_loop(0, shards_n, begin, 0)
    lax.fori_loop(0, shards_n, finish, 0)


def smem():
    return pl.BlockSpec(memory_space=pltpu.SMEM)


def shards(streams, load_counts, seg_ids, rates, residues, skip):
    capacity, _, width = streams.shape
    groups = lax.axis_size("ch")
    spans = lax.axis_size("ctx")
    channels, modes = rates.shape
    length = seg_ids.shape[0]
    rows = width // LANES
    sub = channels // LANES
    mine = lax.axis_index("ch")
    span = lax.axis_index("ctx")

    rate_rows = rates.T
    packed = jnp.concatenate([rate_rows, residues.T, skip[None]], axis=0)
    every = lax.all_gather(packed, "ch")
    every = every.reshape(groups, 2 * modes + 1, sub, LANES).transpose(1, 0, 2, 3).reshape(2 * modes + 1, rows, LANES)
    rate_all = every[:modes]
    decay = jnp.exp(-rate_all)
    weight = every[modes:2 * modes] * jnp.sqrt(-jnp.expm1(-2.0 * rate_all))
    skip_all = every[2 * modes]

    loaded = jnp.transpose(streams.reshape(capacity, 3, rows, LANES), (1, 0, 2, 3))

    counts = load_counts[0]
    ending = jnp.cumsum(counts)
    starts = ending - counts
    count = lax.dynamic_slice(counts, (mine,), (1,))
    start = lax.dynamic_slice(starts, (mine,), (1,))[0]
    same = jnp.concatenate([jnp.ones((1,), jnp.int32), (seg_ids[1:] == seg_ids[:-1]).astype(jnp.int32)])
    row = jnp.arange(capacity, dtype=jnp.int32)
    own = lax.dynamic_slice(jnp.concatenate([same, jnp.ones((capacity,), jnp.int32)]), (start,), (capacity,))
    own = jnp.where(row == 0, 1, own)
    slow = ((own == 0) | (row >= count[0])).reshape(capacity // GROUP, GROUP).any(axis=1).astype(jnp.int32)
    keep = own.astype(F32)

    steps = capacity // TILE
    stream_of = lambda i: pl.BlockSpec((1, TILE, rows, LANES), lambda b: (i, b, 0, 0))
    fixed = lambda *shape: pl.BlockSpec(shape, lambda b: (0,) * len(shape))
    local_end = pl.pallas_call(
        functools.partial(end_state_kernel, modes),
        grid=(steps,),
        out_shape=jax.ShapeDtypeStruct((modes, rows, LANES), F32),
        in_specs=[smem(), smem(), smem(), stream_of(1), stream_of(2), fixed(modes, rows, LANES)],
        out_specs=fixed(modes, rows, LANES),
        compiler_params=pltpu.CompilerParams(vmem_limit_bytes=32 << 20),
    )(count, keep, slow, loaded, loaded, decay)

    outgoing = local_end.reshape(modes, groups, channels).transpose(1, 0, 2)
    ends = lax.all_to_all(outgoing, "ch", split_axis=0, concat_axis=0, tiled=True)

    position = jnp.arange(length, dtype=jnp.int32)
    in_shard = (position[None] >= starts[:, None]) & (position[None] < ending[:, None])
    broken = jnp.any(in_shard & (same[None] == 0), axis=1)
    joins = jnp.any((position[None] == starts[:, None]) & (same[None] == 1), axis=1).astype(F32)
    through = jnp.where(broken, 0.0, 1.0)
    factor = through[:, None, None] * jnp.exp(-counts.astype(F32)[:, None, None] * rate_rows[None])
    ahead, reach = [jnp.zeros_like(rate_rows)], [jnp.ones_like(rate_rows)]
    for j in range(groups):
        ahead.append(factor[j] * ahead[-1] + ends[j])
        reach.append(factor[j] * reach[-1])
    edges = jnp.zeros((1, channels), F32)
    lane = jnp.arange(channels)[None]
    edges = jnp.where(lane == 0, seg_ids[0].astype(F32), jnp.where(lane == 1, seg_ids[-1].astype(F32), 0.0))
    told = lax.all_gather(jnp.concatenate([ahead[-1], edges], axis=0), "ctx")
    span_decay = jnp.exp(-float(length) * rate_rows)
    state_in = jnp.zeros_like(rate_rows)
    arriving = jnp.zeros_like(rate_rows)
    for i in range(spans):
        if i > 0:
            joined = (told[i, modes, 0] == told[i - 1, modes, 1]).astype(F32)
            arriving = joined * arriving
        state_in = jnp.where(span == i, arriving, state_in)
        whole = (told[i, modes, 0] == told[i, modes, 1]).astype(F32)
        arriving = told[i, :modes] + whole * span_decay * arriving
    returning = jnp.stack([joins[j] * (ahead[j] + reach[j] * state_in) for j in range(groups)])
    init = lax.all_to_all(returning, "ch", split_axis=0, concat_axis=0, tiled=True)
    init = init.transpose(1, 0, 2).reshape(modes, rows, LANES)

    mixed = pl.pallas_call(
        functools.partial(mix_kernel, modes),
        grid=(steps,),
        out_shape=jax.ShapeDtypeStruct((rows // 2, capacity, 2, LANES), BF16),
        in_specs=[smem(), smem(), smem(), stream_of(0), stream_of(1), stream_of(2)]
        + [fixed(modes, rows, LANES), fixed(modes, rows, LANES), fixed(rows, LANES), fixed(modes, rows, LANES)],
        out_specs=pl.BlockSpec((rows // 2, TILE, 2, LANES), lambda b: (0, b, 0, 0)),
        scratch_shapes=[pltpu.VMEM((modes, rows, LANES), F32)],
        compiler_params=pltpu.CompilerParams(vmem_limit_bytes=32 << 20),
    )(count, keep, slow, loaded, loaded, loaded, decay, weight, skip_all, init)

    arrived = lax.all_to_all(mixed, "ch", split_axis=0, concat_axis=0, tiled=True)

    bits = capacity.bit_length()
    placed = pl.pallas_call(
        functools.partial(pack_kernel, bits),
        out_shape=jax.ShapeDtypeStruct((length, sub, LANES), BF16),
        in_specs=[smem(), smem(), pl.BlockSpec(memory_space=pl.ANY)],
        out_specs=pl.BlockSpec(memory_space=pl.ANY),
        scratch_shapes=[pltpu.SemaphoreType.DMA((groups, bits))],
    )(counts, starts, arrived)
    return placed.reshape(length, channels)


def solution(mesh):
    return jax.shard_map(
        shards,
        mesh=mesh,
        in_specs=(
            P(("ctx", "ch"), None, None),
            P("ctx", None),
            P("ctx"),
            P("ch", None),
            P("ch", None),
            P("ch"),
        ),
        out_specs=P("ctx", "ch"),
        check_vma=False,
    )
```

```python
import functools

import jax
import jax.numpy as jnp
from jax import lax
from jax.experimental import pallas as pl
from jax.experimental.pallas import tpu as pltpu
from jax.sharding import PartitionSpec as P

LANES = 128
GROUP = 8
TILE = 64
PIECE = 32
MESH = pl.DeviceIdType.MESH
F32 = jnp.float32
BF16 = jnp.bfloat16


def product(k, v):
    return (k.astype(F32) * v.astype(F32)).astype(BF16).astype(F32)


def end_state_kernel(modes, count_ref, keep_ref, slow_ref, k_ref, v_ref, decay_ref, state_ref):
    block = pl.program_id(0)
    rows = k_ref.shape[2]
    count = count_ref[0]

    @pl.when(block == 0)
    def _():
        state_ref[...] = jnp.zeros_like(state_ref)

    def group(r, slow):
        at = pl.ds(r, GROUP)
        x = product(k_ref[0, at], v_ref[0, at])
        first = block * TILE + r
        for h in range(0, rows, 8):
            s = [state_ref[n, h:h + 8] for n in range(modes)]
            d = [decay_ref[n, h:h + 8] for n in range(modes)]
            for t in range(GROUP):
                xt = x[t, h:h + 8]
                if slow:
                    kept = keep_ref[first + t]
                    inside = first + t < count
                    s = [jnp.where(inside, s[n] * (d[n] * kept) + xt, s[n]) for n in range(modes)]
                else:
                    s = [s[n] * d[n] + xt for n in range(modes)]
            for n in range(modes):
                state_ref[n, h:h + 8] = s[n]

    def step(g, carry):
        r = pl.multiple_of(g * GROUP, GROUP)
        is_slow = slow_ref[block * (TILE // GROUP) + g] != 0

        @pl.when(is_slow)
        def _():
            group(r, True)

        @pl.when(jnp.logical_not(is_slow))
        def _():
            group(r, False)

        return carry

    todo = jnp.clip((count - block * TILE + GROUP - 1) // GROUP, 0, TILE // GROUP)
    lax.fori_loop(0, todo, step, 0)


def greet(peers):
    barrier = pltpu.get_barrier_semaphore()
    for peer in peers:
        pl.semaphore_signal(barrier, inc=1, device_id=peer, device_id_type=MESH)
    pl.semaphore_wait(barrier, len(peers))


def around(axis, count, offset):
    return {axis: lax.rem(lax.axis_index(axis) + offset, count)}


def gather_kernel(groups, in_ref, out_ref, send_sem, recv_sem):
    me = lax.axis_index("ch")
    greet([around("ch", groups, off) for off in range(1, groups)])
    copies = []
    for off in range(1, groups):
        copy = pltpu.make_async_remote_copy(
            src_ref=in_ref,
            dst_ref=out_ref.at[me],
            send_sem=send_sem.at[off],
            recv_sem=recv_sem.at[off],
            device_id=around("ch", groups, off),
            device_id_type=MESH,
        )
        copy.start()
        copies.append(copy)
    out_ref[me] = in_ref[...]
    for copy in copies:
        copy.wait()


def exchange_kernel(groups, spans, modes, ends_ref, factor_ref, joins_ref, edges_ref, span_decay_ref, out_ref, got, ahead, reach, told, back, send_sem, recv_sem):
    me = lax.axis_index("ch")
    span = lax.axis_index("ctx")
    others = [around("ch", groups, off) for off in range(1, groups)]
    elsewhere = [around("ctx", spans, off) for off in range(1, spans)]
    greet(others + elsewhere)

    def sent(src, dst, number, peer):
        copy = pltpu.make_async_remote_copy(
            src_ref=src,
            dst_ref=dst,
            send_sem=send_sem.at[number],
            recv_sem=recv_sem.at[number],
            device_id=peer,
            device_id_type=MESH,
        )
        copy.start()
        return copy

    copies = [sent(ends_ref.at[peer["ch"]], got.at[me], i, peer) for i, peer in enumerate(others)]
    got[me] = ends_ref[me]
    for copy in copies:
        copy.wait()
    state = jnp.zeros(got.shape[1:], F32)
    passing = jnp.ones(got.shape[1:], F32)
    for j in range(groups):
        ahead[j] = state
        reach[j] = passing
        state = factor_ref[j] * state + got[j]
        passing = factor_ref[j] * passing
    told[span, 0:modes] = state
    told[span, modes:modes + 8] = edges_ref[...]
    copies = [sent(told.at[span], told.at[span], groups + i, peer) for i, peer in enumerate(elsewhere)]
    for copy in copies:
        copy.wait()
    state_in = jnp.zeros(got.shape[1:], F32)
    arriving = jnp.zeros(got.shape[1:], F32)
    for i in range(spans):
        initial, last = told[i, modes:modes + 1], told[i, modes + 1:modes + 2]
        if i > 0:
            arriving = jnp.where(initial == told[i - 1, modes + 1:modes + 2], 1.0, 0.0) * arriving
        state_in = jnp.where(span == i, arriving, state_in)
        arriving = told[i, 0:modes] + jnp.where(initial == last, 1.0, 0.0) * span_decay_ref[...] * arriving
    for j in range(groups):
        back[j] = joins_ref[j, 0:1] * (ahead[j] + reach[j] * state_in)
    copies = [sent(back.at[peer["ch"]], out_ref.at[me], groups + spans + i, peer) for i, peer in enumerate(others)]
    out_ref[me] = back[me]
    for copy in copies:
        copy.wait()


def mix_kernel(groups, modes, keep_ref, loaded_ref, decay_ref, weight_ref, skip_ref, init_ref, out_ref, state_ref, held, send_sem, recv_sem, own_sem):
    me = lax.axis_index("ch")
    capacity, rows = loaded_ref.shape[1:3]
    greet([around("ch", groups, off) for off in range(1, groups)])
    state_ref[...] = init_ref[...]

    def group(first):
        at = pl.ds(first, GROUP)
        x = product(loaded_ref[1, at], loaded_ref[2, at])
        q = loaded_ref[0, at].astype(F32)
        parts = []
        for h in range(0, rows, 8):
            s = [state_ref[n, h:h + 8] for n in range(modes)]
            d = [decay_ref[n, h:h + 8] for n in range(modes)]
            w = [weight_ref[n, h:h + 8] for n in range(modes)]
            skip = skip_ref[h:h + 8]
            mixed = []
            for t in range(GROUP):
                xt = x[t, h:h + 8]
                kept = keep_ref[first + t]
                s = [s[n] * (d[n] * kept) + xt for n in range(modes)]
                terms = [s[n] * w[n] for n in range(modes)]
                while len(terms) > 1:
                    terms = [a + b for a, b in zip(terms[::2], terms[1::2])]
                mixed.append(q[t, h:h + 8] * (terms[0] + skip * xt))
            for n in range(modes):
                state_ref[n, h:h + 8] = s[n]
            parts.append(mixed)
        for t in range(GROUP):
            whole = jnp.concatenate([part[t] for part in parts], axis=0).astype(BF16)
            for g in range(groups):
                held[g, first + t] = whole[2 * g:2 * g + 2]

    def copy_of(off, at):
        peer = around("ch", groups, off)
        return pltpu.make_async_remote_copy(
            src_ref=held.at[peer["ch"], at],
            dst_ref=out_ref.at[me, at],
            send_sem=send_sem.at[off],
            recv_sem=recv_sem.at[off],
            device_id=peer,
            device_id_type=MESH,
        )

    def block(b, carry):
        def step(g, inner):
            group(b * PIECE + g * GROUP)
            return inner

        lax.fori_loop(0, PIECE // GROUP, step, 0)
        at = pl.ds(b * PIECE, PIECE)
        for off in range(1, groups):
            copy_of(off, at).start()
        return carry

    lax.fori_loop(0, capacity // PIECE, block, 0)
    own = pltpu.make_async_copy(held.at[me], out_ref.at[me], own_sem)
    own.start()
    for off in range(1, groups):
        copy_of(off, pl.ds(0, capacity)).wait()
    own.wait()


def pack_kernel(counts_ref, starts_ref, in_ref, out_ref):
    def shard(j, carry):
        def step(i, inner):
            m = i * GROUP
            out_ref[pl.ds(starts_ref[j] + m, GROUP)] = in_ref[j, pl.ds(m, GROUP)]
            return inner

        lax.fori_loop(0, (counts_ref[j] + GROUP - 1) // GROUP, step, 0)
        return carry

    lax.fori_loop(0, in_ref.shape[0], shard, 0)


def smem():
    return pl.BlockSpec(memory_space=pltpu.SMEM)


def shards(streams, load_counts, seg_ids, rates, residues, skip):
    capacity, _, width = streams.shape
    groups = lax.axis_size("ch")
    spans = lax.axis_size("ctx")
    channels, modes = rates.shape
    length = seg_ids.shape[0]
    rows = width // LANES
    sub = channels // LANES
    mine = lax.axis_index("ch")
    span = lax.axis_index("ctx")

    rate_rows = rates.T
    packed = jnp.concatenate([rate_rows, residues.T, skip[None]], axis=0)
    vmem = pl.BlockSpec(memory_space=pltpu.VMEM)
    every = pl.pallas_call(
        functools.partial(gather_kernel, groups),
        out_shape=jax.ShapeDtypeStruct((groups,) + packed.shape, F32),
        in_specs=[vmem],
        out_specs=vmem,
        scratch_shapes=[pltpu.SemaphoreType.DMA((groups,)), pltpu.SemaphoreType.DMA((groups,))],
        compiler_params=pltpu.CompilerParams(collective_id=0, has_side_effects=True, vmem_limit_bytes=16 << 20),
    )(packed)
    every = every.reshape(groups, 2 * modes + 1, sub, LANES).transpose(1, 0, 2, 3).reshape(2 * modes + 1, rows, LANES)
    rate_all = every[:modes]
    decay = jnp.exp(-rate_all)
    weight = every[modes:2 * modes] * jnp.sqrt(-jnp.expm1(-2.0 * rate_all))
    skip_all = every[2 * modes]

    loaded = jnp.transpose(streams.reshape(capacity, 3, rows, LANES), (1, 0, 2, 3))

    counts = load_counts[0]
    ending = jnp.cumsum(counts)
    starts = ending - counts
    count = lax.dynamic_slice(counts, (mine,), (1,))
    start = lax.dynamic_slice(starts, (mine,), (1,))[0]
    same = jnp.concatenate([jnp.ones((1,), jnp.int32), (seg_ids[1:] == seg_ids[:-1]).astype(jnp.int32)])
    row = jnp.arange(capacity, dtype=jnp.int32)
    own = lax.dynamic_slice(jnp.concatenate([same, jnp.ones((capacity,), jnp.int32)]), (start,), (capacity,))
    own = jnp.where(row == 0, 1, own)
    slow = ((own == 0) | (row >= count[0])).reshape(capacity // GROUP, GROUP).any(axis=1).astype(jnp.int32)
    keep = own.astype(F32)

    steps = capacity // TILE
    stream_of = lambda i: pl.BlockSpec((1, TILE, rows, LANES), lambda b: (i, b, 0, 0))
    fixed = lambda *shape: pl.BlockSpec(shape, lambda b: (0,) * len(shape))
    local_end = pl.pallas_call(
        functools.partial(end_state_kernel, modes),
        grid=(steps,),
        out_shape=jax.ShapeDtypeStruct((modes, rows, LANES), F32),
        in_specs=[smem(), smem(), smem(), stream_of(1), stream_of(2), fixed(modes, rows, LANES)],
        out_specs=fixed(modes, rows, LANES),
        compiler_params=pltpu.CompilerParams(vmem_limit_bytes=32 << 20),
    )(count, keep, slow, loaded, loaded, decay)

    outgoing = local_end.reshape(modes, groups, channels).transpose(1, 0, 2)

    position = jnp.arange(length, dtype=jnp.int32)
    in_shard = (position[None] >= starts[:, None]) & (position[None] < ending[:, None])
    broken = jnp.any(in_shard & (same[None] == 0), axis=1)
    joins = jnp.any((position[None] == starts[:, None]) & (same[None] == 1), axis=1).astype(F32)
    through = jnp.where(broken, 0.0, 1.0)
    factor = through[:, None, None] * jnp.exp(-counts.astype(F32)[:, None, None] * rate_rows[None])
    edges = jnp.broadcast_to(jnp.concatenate([seg_ids[:1], jnp.tile(seg_ids[-1:], 7)]).astype(F32)[:, None], (8, channels))
    span_decay = jnp.exp(-float(length) * rate_rows)
    joins_wide = jnp.broadcast_to(joins[:, None, None], (groups, 8, channels))
    flat = pltpu.VMEM((groups, modes, channels), F32)
    slots = 2 * groups + spans
    init = pl.pallas_call(
        functools.partial(exchange_kernel, groups, spans, modes),
        out_shape=jax.ShapeDtypeStruct((groups, modes, channels), F32),
        in_specs=[vmem] * 5,
        out_specs=vmem,
        scratch_shapes=[
            flat,
            flat,
            flat,
            pltpu.VMEM((spans, modes + 8, channels), F32),
            flat,
            pltpu.SemaphoreType.DMA((slots,)),
            pltpu.SemaphoreType.DMA((slots,)),
        ],
        compiler_params=pltpu.CompilerParams(collective_id=1, has_side_effects=True, vmem_limit_bytes=32 << 20),
    )(outgoing, factor, joins_wide, edges, span_decay)
    init = init.transpose(1, 0, 2).reshape(modes, rows, LANES)

    arrived = pl.pallas_call(
        functools.partial(mix_kernel, groups, modes),
        out_shape=jax.ShapeDtypeStruct((groups, capacity, sub, LANES), BF16),
        in_specs=[smem()] + [vmem] * 5,
        out_specs=vmem,
        scratch_shapes=[
            pltpu.VMEM((modes, rows, LANES), F32),
            pltpu.VMEM((groups, capacity, sub, LANES), BF16),
            pltpu.SemaphoreType.DMA((groups,)),
            pltpu.SemaphoreType.DMA((groups,)),
            pltpu.SemaphoreType.DMA,
        ],
        compiler_params=pltpu.CompilerParams(collective_id=2, has_side_effects=True, vmem_limit_bytes=40 << 20),
    )(keep, loaded, decay, weight, skip_all, init)

    placed = pl.pallas_call(
        pack_kernel,
        out_shape=jax.ShapeDtypeStruct((length + GROUP, sub, LANES), BF16),
        in_specs=[smem(), smem(), vmem],
        out_specs=vmem,
        compiler_params=pltpu.CompilerParams(vmem_limit_bytes=32 << 20),
    )(counts, starts, arrived)
    return placed[:length].reshape(length, channels)


def solution(mesh):
    return jax.shard_map(
        shards,
        mesh=mesh,
        in_specs=(
            P(("ctx", "ch"), None, None),
            P("ctx", None),
            P("ctx"),
            P("ch", None),
            P("ch", None),
            P("ch"),
        ),
        out_specs=P("ctx", "ch"),
        check_vma=False,
    )
```

```python
import functools

import jax
import jax.numpy as jnp
from jax import lax
from jax.experimental import pallas as pl
from jax.experimental.pallas import tpu as pltpu
from jax.sharding import PartitionSpec as P

LANES = 128
GROUP = 8
TILE = 64
PIECE = 32
MESH = pl.DeviceIdType.MESH
F32 = jnp.float32
BF16 = jnp.bfloat16


def product(k, v):
    return (k.astype(F32) * v.astype(F32)).astype(BF16).astype(F32)


def own_rows(counts_ref, number):
    me = lax.axis_index("ch")
    start = jnp.int32(0)
    for j in range(number):
        start = start + jnp.where(j < me, counts_ref[j], 0)
    return start


def kept_rows(seg_ref, start, first):
    last = seg_ref.shape[0] - 1
    ids = [seg_ref[jnp.clip(start + first + t, 0, last)] for t in range(-1, GROUP)]
    kept = [jnp.where(a == b, 1.0, 0.0).astype(F32) for a, b in zip(ids, ids[1:])]
    kept[0] = jnp.where(first == 0, 1.0, kept[0])
    return kept


def end_state_kernel(modes, groups, counts_ref, seg_ref, k_ref, v_ref, decay_ref, state_ref):
    block = pl.program_id(0)
    rows = k_ref.shape[2]
    count = counts_ref[lax.axis_index("ch")]
    start = own_rows(counts_ref, groups)
    last = seg_ref.shape[0] - 1

    @pl.when(block == 0)
    def _():
        state_ref[...] = jnp.zeros_like(state_ref)

    def group(r, slow):
        at = pl.ds(r, GROUP)
        x = product(k_ref[0, at], v_ref[0, at])
        first = block * TILE + r
        kept = kept_rows(seg_ref, start, first) if slow else None
        for h in range(0, rows, 8):
            s = [state_ref[n, h:h + 8] for n in range(modes)]
            d = [decay_ref[n, h:h + 8] for n in range(modes)]
            for t in range(GROUP):
                xt = x[t, h:h + 8]
                if slow:
                    inside = first + t < count
                    s = [jnp.where(inside, s[n] * (d[n] * kept[t]) + xt, s[n]) for n in range(modes)]
                else:
                    s = [s[n] * d[n] + xt for n in range(modes)]
            for n in range(modes):
                state_ref[n, h:h + 8] = s[n]

    def step(g, carry):
        r = pl.multiple_of(g * GROUP, GROUP)
        begin = start + block * TILE + r
        before = seg_ref[jnp.maximum(begin - 1, 0)]
        after = seg_ref[jnp.minimum(begin + GROUP - 1, last)]
        is_slow = (before != after) | (block * TILE + r + GROUP > count)

        @pl.when(is_slow)
        def _():
            group(r, True)

        @pl.when(jnp.logical_not(is_slow))
        def _():
            group(r, False)

        return carry

    todo = jnp.clip((count - block * TILE + GROUP - 1) // GROUP, 0, TILE // GROUP)
    lax.fori_loop(0, todo, step, 0)


def greet(peers):
    barrier = pltpu.get_barrier_semaphore()
    for peer in peers:
        pl.semaphore_signal(barrier, inc=1, device_id=peer, device_id_type=MESH)
    pl.semaphore_wait(barrier, len(peers))


def around(axis, count, offset):
    return {axis: lax.rem(lax.axis_index(axis) + offset, count)}


def gather_kernel(groups, in_ref, out_ref, send_sem, recv_sem):
    me = lax.axis_index("ch")
    greet([around("ch", groups, off) for off in range(1, groups)])
    copies = []
    for off in range(1, groups):
        copy = pltpu.make_async_remote_copy(
            src_ref=in_ref,
            dst_ref=out_ref.at[me],
            send_sem=send_sem.at[off],
            recv_sem=recv_sem.at[off],
            device_id=around("ch", groups, off),
            device_id_type=MESH,
        )
        copy.start()
        copies.append(copy)
    out_ref[me] = in_ref[...]
    for copy in copies:
        copy.wait()


def exchange_kernel(groups, spans, modes, counts_ref, seg_ref, ends_ref, rate_ref, out_ref, got, ahead, reach, told, back, send_sem, recv_sem):
    me = lax.axis_index("ch")
    span = lax.axis_index("ctx")
    others = [around("ch", groups, off) for off in range(1, groups)]
    elsewhere = [around("ctx", spans, off) for off in range(1, spans)]
    greet(others + elsewhere)

    def sent(src, dst, number, peer):
        copy = pltpu.make_async_remote_copy(
            src_ref=src,
            dst_ref=dst,
            send_sem=send_sem.at[number],
            recv_sem=recv_sem.at[number],
            device_id=peer,
            device_id_type=MESH,
        )
        copy.start()
        return copy

    copies = [sent(ends_ref.at[peer["ch"]], got.at[me], i, peer) for i, peer in enumerate(others)]
    got[me] = ends_ref[me]
    for copy in copies:
        copy.wait()
    length = seg_ref.shape[0]
    first_id, last_id = seg_ref[0], seg_ref[length - 1]
    rate = rate_ref[...]
    state = jnp.zeros(got.shape[1:], F32)
    passing = jnp.ones(got.shape[1:], F32)
    joins = []
    start, before = jnp.int32(0), first_id
    for j in range(groups):
        joins.append(jnp.where(seg_ref[jnp.clip(start, 0, length - 1)] == before, 1.0, 0.0).astype(F32))
        start = start + counts_ref[j]
        after = seg_ref[jnp.clip(start - 1, 0, length - 1)]
        through = jnp.where(before == after, 1.0, 0.0).astype(F32)
        factor = jnp.exp(rate * -counts_ref[j].astype(F32)) * through
        ahead[j] = state
        reach[j] = passing
        state = factor * state + got[j]
        passing = factor * passing
        before = after
    span_decay = jnp.exp(rate * -float(length))
    wide = (8, got.shape[2])
    row = lax.broadcasted_iota(jnp.int32, wide, 0)
    edges = jnp.where(row == 0, jnp.full(wide, first_id.astype(F32)), jnp.full(wide, last_id.astype(F32)))
    told[span, 0:modes] = state
    told[span, modes:modes + 8] = edges
    copies = [sent(told.at[span], told.at[span], groups + i, peer) for i, peer in enumerate(elsewhere)]
    for copy in copies:
        copy.wait()
    state_in = jnp.zeros(got.shape[1:], F32)
    arriving = jnp.zeros(got.shape[1:], F32)
    for i in range(spans):
        initial, last = told[i, modes:modes + 1], told[i, modes + 1:modes + 2]
        if i > 0:
            arriving = jnp.where(initial == told[i - 1, modes + 1:modes + 2], 1.0, 0.0) * arriving
        state_in = jnp.where(span == i, arriving, state_in)
        arriving = told[i, 0:modes] + jnp.where(initial == last, 1.0, 0.0) * span_decay * arriving
    for j in range(groups):
        back[j] = joins[j] * (ahead[j] + reach[j] * state_in)
    copies = [sent(back.at[peer["ch"]], out_ref.at[me], groups + spans + i, peer) for i, peer in enumerate(others)]
    out_ref[me] = back[me]
    for copy in copies:
        copy.wait()


def mix_kernel(groups, modes, counts_ref, seg_ref, loaded_ref, decay_ref, weight_ref, skip_ref, init_ref, out_ref, state_ref, held, send_sem, recv_sem, own_sem):
    me = lax.axis_index("ch")
    capacity, rows = loaded_ref.shape[1:3]
    greet([around("ch", groups, off) for off in range(1, groups)])
    state_ref[...] = init_ref[...]
    start = own_rows(counts_ref, groups)

    def group(first):
        kept = kept_rows(seg_ref, start, first)
        at = pl.ds(first, GROUP)
        x = product(loaded_ref[1, at], loaded_ref[2, at])
        q = loaded_ref[0, at].astype(F32)
        parts = []
        for h in range(0, rows, 8):
            s = [state_ref[n, h:h + 8] for n in range(modes)]
            d = [decay_ref[n, h:h + 8] for n in range(modes)]
            w = [weight_ref[n, h:h + 8] for n in range(modes)]
            skip = skip_ref[h:h + 8]
            mixed = []
            for t in range(GROUP):
                xt = x[t, h:h + 8]
                s = [s[n] * (d[n] * kept[t]) + xt for n in range(modes)]
                terms = [s[n] * w[n] for n in range(modes)]
                while len(terms) > 1:
                    terms = [a + b for a, b in zip(terms[::2], terms[1::2])]
                mixed.append(q[t, h:h + 8] * (terms[0] + skip * xt))
            for n in range(modes):
                state_ref[n, h:h + 8] = s[n]
            parts.append(mixed)
        for t in range(GROUP):
            whole = jnp.concatenate([part[t] for part in parts], axis=0).astype(BF16)
            for g in range(groups):
                held[g, first + t] = whole[2 * g:2 * g + 2]

    def copy_of(off, at):
        peer = around("ch", groups, off)
        return pltpu.make_async_remote_copy(
            src_ref=held.at[peer["ch"], at],
            dst_ref=out_ref.at[me, at],
            send_sem=send_sem.at[off],
            recv_sem=recv_sem.at[off],
            device_id=peer,
            device_id_type=MESH,
        )

    def block(b, carry):
        def step(g, inner):
            group(b * PIECE + g * GROUP)
            return inner

        lax.fori_loop(0, PIECE // GROUP, step, 0)
        at = pl.ds(b * PIECE, PIECE)
        for off in range(1, groups):
            copy_of(off, at).start()
        return carry

    lax.fori_loop(0, capacity // PIECE, block, 0)
    own = pltpu.make_async_copy(held.at[me], out_ref.at[me], own_sem)
    own.start()
    for off in range(1, groups):
        copy_of(off, pl.ds(0, capacity)).wait()
    own.wait()


def pack_kernel(counts_ref, in_ref, out_ref):
    def shard(j, start):
        def step(i, inner):
            m = i * GROUP
            out_ref[pl.ds(start + m, GROUP)] = in_ref[j, pl.ds(m, GROUP)]
            return inner

        lax.fori_loop(0, (counts_ref[j] + GROUP - 1) // GROUP, step, 0)
        return start + counts_ref[j]

    lax.fori_loop(0, in_ref.shape[0], shard, jnp.int32(0))


def smem():
    return pl.BlockSpec(memory_space=pltpu.SMEM)


def shards(streams, load_counts, seg_ids, rates, residues, skip):
    capacity, _, width = streams.shape
    groups = lax.axis_size("ch")
    spans = lax.axis_size("ctx")
    channels, modes = rates.shape
    length = seg_ids.shape[0]
    rows = width // LANES
    sub = channels // LANES

    rate_rows = rates.T
    gain = jnp.sqrt(-jnp.expm1(-2.0 * rate_rows))
    packed = jnp.concatenate([jnp.exp(-rate_rows), residues.T * gain, skip[None]], axis=0)
    vmem = pl.BlockSpec(memory_space=pltpu.VMEM)
    every = pl.pallas_call(
        functools.partial(gather_kernel, groups),
        out_shape=jax.ShapeDtypeStruct((groups,) + packed.shape, F32),
        in_specs=[vmem],
        out_specs=vmem,
        scratch_shapes=[pltpu.SemaphoreType.DMA((groups,)), pltpu.SemaphoreType.DMA((groups,))],
        compiler_params=pltpu.CompilerParams(collective_id=0, has_side_effects=True, vmem_limit_bytes=6 << 20),
    )(packed)
    every = every.reshape(groups, 2 * modes + 1, sub, LANES).transpose(1, 0, 2, 3).reshape(2 * modes + 1, rows, LANES)
    decay, weight, skip_all = every[:modes], every[modes:2 * modes], every[2 * modes]

    loaded = jnp.transpose(streams.reshape(capacity, 3, rows, LANES), (1, 0, 2, 3))

    counts = load_counts[0]
    steps = capacity // TILE
    stream_of = lambda i: pl.BlockSpec((1, TILE, rows, LANES), lambda b: (i, b, 0, 0))
    fixed = lambda *shape: pl.BlockSpec(shape, lambda b: (0,) * len(shape))
    local_end = pl.pallas_call(
        functools.partial(end_state_kernel, modes, groups),
        grid=(steps,),
        out_shape=jax.ShapeDtypeStruct((modes, rows, LANES), F32),
        in_specs=[smem(), smem(), stream_of(1), stream_of(2), fixed(modes, rows, LANES)],
        out_specs=fixed(modes, rows, LANES),
        compiler_params=pltpu.CompilerParams(vmem_limit_bytes=6 << 20),
    )(counts, seg_ids, loaded, loaded, decay)

    outgoing = local_end.reshape(modes, groups, channels).transpose(1, 0, 2)

    flat = pltpu.VMEM((groups, modes, channels), F32)
    slots = 2 * groups + spans
    init = pl.pallas_call(
        functools.partial(exchange_kernel, groups, spans, modes),
        out_shape=jax.ShapeDtypeStruct((groups, modes, channels), F32),
        in_specs=[smem(), smem(), vmem, vmem],
        out_specs=vmem,
        scratch_shapes=[
            flat,
            flat,
            flat,
            pltpu.VMEM((spans, modes + 8, channels), F32),
            flat,
            pltpu.SemaphoreType.DMA((slots,)),
            pltpu.SemaphoreType.DMA((slots,)),
        ],
        compiler_params=pltpu.CompilerParams(collective_id=1, has_side_effects=True, vmem_limit_bytes=8 << 20),
    )(counts, seg_ids, outgoing, rate_rows)
    init = init.transpose(1, 0, 2).reshape(modes, rows, LANES)

    arrived = pl.pallas_call(
        functools.partial(mix_kernel, groups, modes),
        out_shape=jax.ShapeDtypeStruct((groups, capacity, sub, LANES), BF16),
        in_specs=[smem(), smem()] + [vmem] * 5,
        out_specs=vmem,
        scratch_shapes=[
            pltpu.VMEM((modes, rows, LANES), F32),
            pltpu.VMEM((groups, capacity, sub, LANES), BF16),
            pltpu.SemaphoreType.DMA((groups,)),
            pltpu.SemaphoreType.DMA((groups,)),
            pltpu.SemaphoreType.DMA,
        ],
        compiler_params=pltpu.CompilerParams(collective_id=2, has_side_effects=True, vmem_limit_bytes=20 << 20),
    )(counts, seg_ids, loaded, decay, weight, skip_all, init)

    placed = pl.pallas_call(
        pack_kernel,
        out_shape=jax.ShapeDtypeStruct((length + GROUP, sub, LANES), BF16),
        in_specs=[smem(), vmem],
        out_specs=vmem,
        compiler_params=pltpu.CompilerParams(vmem_limit_bytes=16 << 20),
    )(counts, arrived)
    return placed[:length].reshape(length, channels)


def solution(mesh):
    return jax.shard_map(
        shards,
        mesh=mesh,
        in_specs=(
            P(("ctx", "ch"), None, None),
            P("ctx", None),
            P("ctx"),
            P("ch", None),
            P("ch", None),
            P("ch"),
        ),
        out_specs=P("ctx", "ch"),
        check_vma=False,
    )
```

```python
import functools

import jax
import jax.numpy as jnp
from jax import lax
from jax.experimental import pallas as pl
from jax.experimental.pallas import tpu as pltpu
from jax.sharding import PartitionSpec as P

LANES = 128
GROUP = 8
TILE = 64
PIECE = 32
MESH = pl.DeviceIdType.MESH
F32 = jnp.float32
BF16 = jnp.bfloat16


def product(k, v):
    return (k.astype(F32) * v.astype(F32)).astype(BF16).astype(F32)


def own_rows(counts_ref, number):
    me = lax.axis_index("ch")
    start = jnp.int32(0)
    for j in range(number):
        start = start + jnp.where(j < me, counts_ref[j], 0)
    return start


def kept_rows(seg_ref, start, first):
    last = seg_ref.shape[0] - 1
    ids = [seg_ref[jnp.clip(start + first + t, 0, last)] for t in range(-1, GROUP)]
    kept = [jnp.where(a == b, 1.0, 0.0).astype(F32) for a, b in zip(ids, ids[1:])]
    kept[0] = jnp.where(first == 0, 1.0, kept[0])
    return kept


def end_state_kernel(modes, groups, counts_ref, seg_ref, k_ref, v_ref, decay_ref, state_ref):
    block = pl.program_id(0)
    rows = k_ref.shape[2]
    count = counts_ref[lax.axis_index("ch")]
    start = own_rows(counts_ref, groups)
    last = seg_ref.shape[0] - 1

    @pl.when(block == 0)
    def _():
        state_ref[...] = jnp.zeros_like(state_ref)

    def group(r, slow):
        at = pl.ds(r, GROUP)
        x = product(k_ref[0, at], v_ref[0, at])
        first = block * TILE + r
        kept = kept_rows(seg_ref, start, first) if slow else None
        for h in range(0, rows, 8):
            s = [state_ref[n, h:h + 8] for n in range(modes)]
            d = [decay_ref[n, h:h + 8] for n in range(modes)]
            for t in range(GROUP):
                xt = x[t, h:h + 8]
                if slow:
                    inside = first + t < count
                    s = [jnp.where(inside, s[n] * (d[n] * kept[t]) + xt, s[n]) for n in range(modes)]
                else:
                    s = [s[n] * d[n] + xt for n in range(modes)]
            for n in range(modes):
                state_ref[n, h:h + 8] = s[n]

    def step(g, carry):
        r = pl.multiple_of(g * GROUP, GROUP)
        begin = start + block * TILE + r
        before = seg_ref[jnp.maximum(begin - 1, 0)]
        after = seg_ref[jnp.minimum(begin + GROUP - 1, last)]
        is_slow = (before != after) | (block * TILE + r + GROUP > count)

        @pl.when(is_slow)
        def _():
            group(r, True)

        @pl.when(jnp.logical_not(is_slow))
        def _():
            group(r, False)

        return carry

    todo = jnp.clip((count - block * TILE + GROUP - 1) // GROUP, 0, TILE // GROUP)
    lax.fori_loop(0, todo, step, 0)


def greet(peers):
    barrier = pltpu.get_barrier_semaphore()
    for peer in peers:
        pl.semaphore_signal(barrier, inc=1, device_id=peer, device_id_type=MESH)
    pl.semaphore_wait(barrier, len(peers))


def around(axis, count, offset):
    return {axis: lax.rem(lax.axis_index(axis) + offset, count)}


def gather_kernel(groups, in_ref, out_ref, send_sem, recv_sem):
    me = lax.axis_index("ch")
    greet([around("ch", groups, off) for off in range(1, groups)])
    copies = []
    for off in range(1, groups):
        copy = pltpu.make_async_remote_copy(
            src_ref=in_ref,
            dst_ref=out_ref.at[me],
            send_sem=send_sem.at[off],
            recv_sem=recv_sem.at[off],
            device_id=around("ch", groups, off),
            device_id_type=MESH,
        )
        copy.start()
        copies.append(copy)
    out_ref[me] = in_ref[...]
    for copy in copies:
        copy.wait()


def mix_kernel(groups, spans, modes, counts_ref, seg_ref, ends_ref, rate_ref, loaded_ref, decay_ref, weight_ref, skip_ref, out_ref, got, ahead, reach, told, back, land, send_sem, recv_sem, state_ref, held, row_send, row_recv, own_sem):
    me = lax.axis_index("ch")
    span = lax.axis_index("ctx")
    others = [around("ch", groups, off) for off in range(1, groups)]
    elsewhere = [around("ctx", spans, off) for off in range(1, spans)]
    greet(others + elsewhere)

    def sent(src, dst, number, peer):
        copy = pltpu.make_async_remote_copy(
            src_ref=src,
            dst_ref=dst,
            send_sem=send_sem.at[number],
            recv_sem=recv_sem.at[number],
            device_id=peer,
            device_id_type=MESH,
        )
        copy.start()
        return copy

    copies = [sent(ends_ref.at[peer["ch"]], got.at[me], i, peer) for i, peer in enumerate(others)]
    got[me] = ends_ref[me]
    for copy in copies:
        copy.wait()
    length = seg_ref.shape[0]
    first_id, last_id = seg_ref[0], seg_ref[length - 1]
    rate = rate_ref[...]
    state = jnp.zeros(got.shape[1:], F32)
    passing = jnp.ones(got.shape[1:], F32)
    joins = []
    start, before = jnp.int32(0), first_id
    for j in range(groups):
        joins.append(jnp.where(seg_ref[jnp.clip(start, 0, length - 1)] == before, 1.0, 0.0).astype(F32))
        start = start + counts_ref[j]
        after = seg_ref[jnp.clip(start - 1, 0, length - 1)]
        through = jnp.where(before == after, 1.0, 0.0).astype(F32)
        factor = jnp.exp(rate * -counts_ref[j].astype(F32)) * through
        ahead[j] = state
        reach[j] = passing
        state = factor * state + got[j]
        passing = factor * passing
        before = after
    span_decay = jnp.exp(rate * -float(length))
    wide = (8, got.shape[2])
    row = lax.broadcasted_iota(jnp.int32, wide, 0)
    edges = jnp.where(row == 0, jnp.full(wide, first_id.astype(F32)), jnp.full(wide, last_id.astype(F32)))
    told[span, 0:modes] = state
    told[span, modes:modes + 8] = edges
    copies = [sent(told.at[span], told.at[span], groups + i, peer) for i, peer in enumerate(elsewhere)]
    for copy in copies:
        copy.wait()
    state_in = jnp.zeros(got.shape[1:], F32)
    arriving = jnp.zeros(got.shape[1:], F32)
    for i in range(spans):
        initial, last = told[i, modes:modes + 1], told[i, modes + 1:modes + 2]
        if i > 0:
            arriving = jnp.where(initial == told[i - 1, modes + 1:modes + 2], 1.0, 0.0) * arriving
        state_in = jnp.where(span == i, arriving, state_in)
        arriving = told[i, 0:modes] + jnp.where(initial == last, 1.0, 0.0) * span_decay * arriving
    for j in range(groups):
        back[j] = joins[j] * (ahead[j] + reach[j] * state_in)
    copies = [sent(back.at[peer["ch"]], land.at[me], groups + spans + i, peer) for i, peer in enumerate(others)]
    land[me] = back[me]
    for copy in copies:
        copy.wait()
    for g in range(groups):
        for h in range(2):
            state_ref[:, 2 * g + h, :] = land[g, :, h * LANES:(h + 1) * LANES]

    capacity, rows = loaded_ref.shape[1:3]
    start = own_rows(counts_ref, groups)
    order = sorted(range(1, groups), key=lambda off: abs(off - groups // 2))

    def group(first):
        kept = kept_rows(seg_ref, start, first)
        at = pl.ds(first, GROUP)
        x = product(loaded_ref[1, at], loaded_ref[2, at])
        q = loaded_ref[0, at].astype(F32)
        parts = []
        for h in range(0, rows, 8):
            s = [state_ref[n, h:h + 8] for n in range(modes)]
            d = [decay_ref[n, h:h + 8] for n in range(modes)]
            w = [weight_ref[n, h:h + 8] for n in range(modes)]
            skip = skip_ref[h:h + 8]
            mixed = []
            for t in range(GROUP):
                xt = x[t, h:h + 8]
                s = [s[n] * (d[n] * kept[t]) + xt for n in range(modes)]
                terms = [s[n] * w[n] for n in range(modes)]
                while len(terms) > 1:
                    terms = [a + b for a, b in zip(terms[::2], terms[1::2])]
                mixed.append(q[t, h:h + 8] * (terms[0] + skip * xt))
            for n in range(modes):
                state_ref[n, h:h + 8] = s[n]
            parts.append(mixed)
        for t in range(GROUP):
            whole = jnp.concatenate([part[t] for part in parts], axis=0).astype(BF16)
            for g in range(groups):
                held[g, first + t] = whole[2 * g:2 * g + 2]

    def copy_of(off, at):
        peer = around("ch", groups, off)
        return pltpu.make_async_remote_copy(
            src_ref=held.at[peer["ch"], at],
            dst_ref=out_ref.at[me, at],
            send_sem=row_send.at[off],
            recv_sem=row_recv.at[off],
            device_id=peer,
            device_id_type=MESH,
        )

    def block(b, carry):
        def step(g, inner):
            group(b * PIECE + g * GROUP)
            return inner

        lax.fori_loop(0, PIECE // GROUP, step, 0)
        at = pl.ds(b * PIECE, PIECE)
        for off in order:
            copy_of(off, at).start()
        return carry

    lax.fori_loop(0, capacity // PIECE, block, 0)
    own = pltpu.make_async_copy(held.at[me], out_ref.at[me], own_sem)
    own.start()
    for off in range(1, groups):
        copy_of(off, pl.ds(0, capacity)).wait()
    own.wait()


def pack_kernel(counts_ref, in_ref, out_ref):
    def shard(j, start):
        count = counts_ref[j]
        even = (count // GROUP) * GROUP

        def step(i, inner):
            m = i * GROUP
            out_ref[pl.ds(start + m, GROUP)] = in_ref[j, pl.ds(m, GROUP)]
            return inner

        def single(m, inner):
            out_ref[pl.ds(start + m, 1)] = in_ref[j, pl.ds(m, 1)]
            return inner

        lax.fori_loop(0, count // GROUP, step, 0)
        lax.fori_loop(even, count, single, 0)
        return start + count

    lax.fori_loop(0, in_ref.shape[0], shard, jnp.int32(0))


def smem():
    return pl.BlockSpec(memory_space=pltpu.SMEM)


def shards(streams, load_counts, seg_ids, rates, residues, skip):
    capacity, _, width = streams.shape
    groups = lax.axis_size("ch")
    spans = lax.axis_size("ctx")
    channels, modes = rates.shape
    length = seg_ids.shape[0]
    rows = width // LANES
    sub = channels // LANES

    rate_rows = rates.T
    gain = jnp.sqrt(-jnp.expm1(-2.0 * rate_rows))
    packed = jnp.concatenate([jnp.exp(-rate_rows), residues.T * gain, skip[None]], axis=0)
    vmem = pl.BlockSpec(memory_space=pltpu.VMEM)
    every = pl.pallas_call(
        functools.partial(gather_kernel, groups),
        out_shape=jax.ShapeDtypeStruct((groups,) + packed.shape, F32),
        in_specs=[vmem],
        out_specs=vmem,
        scratch_shapes=[pltpu.SemaphoreType.DMA((groups,)), pltpu.SemaphoreType.DMA((groups,))],
        compiler_params=pltpu.CompilerParams(collective_id=0, has_side_effects=True, vmem_limit_bytes=6 << 20),
    )(packed)
    every = every.reshape(groups, 2 * modes + 1, sub, LANES).transpose(1, 0, 2, 3).reshape(2 * modes + 1, rows, LANES)
    decay, weight, skip_all = every[:modes], every[modes:2 * modes], every[2 * modes]

    loaded = jnp.transpose(streams.reshape(capacity, 3, rows, LANES), (1, 0, 2, 3))

    counts = load_counts[0]
    steps = capacity // TILE
    stream_of = lambda i: pl.BlockSpec((1, TILE, rows, LANES), lambda b: (i, b, 0, 0))
    fixed = lambda *shape: pl.BlockSpec(shape, lambda b: (0,) * len(shape))
    local_end = pl.pallas_call(
        functools.partial(end_state_kernel, modes, groups),
        grid=(steps,),
        out_shape=jax.ShapeDtypeStruct((modes, rows, LANES), F32),
        in_specs=[smem(), smem(), stream_of(1), stream_of(2), fixed(modes, rows, LANES)],
        out_specs=fixed(modes, rows, LANES),
        compiler_params=pltpu.CompilerParams(vmem_limit_bytes=6 << 20),
    )(counts, seg_ids, loaded, loaded, decay)

    outgoing = local_end.reshape(modes, groups, channels).transpose(1, 0, 2)

    flat = pltpu.VMEM((groups, modes, channels), F32)
    slots = 2 * groups + spans
    arrived = pl.pallas_call(
        functools.partial(mix_kernel, groups, spans, modes),
        out_shape=jax.ShapeDtypeStruct((groups, capacity, sub, LANES), BF16),
        in_specs=[smem(), smem()] + [vmem] * 6,
        out_specs=vmem,
        scratch_shapes=[
            flat,
            flat,
            flat,
            pltpu.VMEM((spans, modes + 8, channels), F32),
            flat,
            flat,
            pltpu.SemaphoreType.DMA((slots,)),
            pltpu.SemaphoreType.DMA((slots,)),
            pltpu.VMEM((modes, rows, LANES), F32),
            pltpu.VMEM((groups, capacity, sub, LANES), BF16),
            pltpu.SemaphoreType.DMA((groups,)),
            pltpu.SemaphoreType.DMA((groups,)),
            pltpu.SemaphoreType.DMA,
        ],
        compiler_params=pltpu.CompilerParams(collective_id=1, has_side_effects=True, vmem_limit_bytes=24 << 20),
    )(counts, seg_ids, outgoing, rate_rows, loaded, decay, weight, skip_all)

    placed = pl.pallas_call(
        pack_kernel,
        out_shape=jax.ShapeDtypeStruct((length, sub, LANES), BF16),
        in_specs=[smem(), vmem],
        out_specs=vmem,
        compiler_params=pltpu.CompilerParams(vmem_limit_bytes=16 << 20),
    )(counts, arrived)
    return placed.reshape(length, channels)


def solution(mesh):
    return jax.shard_map(
        shards,
        mesh=mesh,
        in_specs=(
            P(("ctx", "ch"), None, None),
            P("ctx", None),
            P("ctx"),
            P("ch", None),
            P("ch", None),
            P("ch"),
        ),
        out_specs=P("ctx", "ch"),
        check_vma=False,
    )
```

```python
import functools

import jax
import jax.numpy as jnp
from jax import lax
from jax.experimental import pallas as pl
from jax.experimental.pallas import tpu as pltpu
from jax.sharding import PartitionSpec as P

LANES = 128
GROUP = 8
TILE = 64
PIECE = 32
ROOM = 50 << 20
MESH = pl.DeviceIdType.MESH
F32 = jnp.float32
BF16 = jnp.bfloat16


def product(k, v):
    return (k.astype(F32) * v.astype(F32)).astype(BF16).astype(F32)


def own_rows(counts_ref, number):
    me = lax.axis_index("ch")
    start = jnp.int32(0)
    for j in range(number):
        start = start + jnp.where(j < me, counts_ref[j], 0)
    return start


def kept_rows(seg_ref, start, first):
    last = seg_ref.shape[0] - 1
    ids = [seg_ref[jnp.clip(start + first + t, 0, last)] for t in range(-1, GROUP)]
    kept = [jnp.where(a == b, 1.0, 0.0).astype(F32) for a, b in zip(ids, ids[1:])]
    kept[0] = jnp.where(first == 0, 1.0, kept[0])
    return kept


def end_state_kernel(modes, groups, counts_ref, seg_ref, k_ref, v_ref, decay_ref, state_ref):
    block = pl.program_id(0)
    rows = k_ref.shape[2]
    count = counts_ref[lax.axis_index("ch")]
    start = own_rows(counts_ref, groups)
    last = seg_ref.shape[0] - 1

    @pl.when(block == 0)
    def _():
        state_ref[...] = jnp.zeros_like(state_ref)

    def group(r, slow):
        at = pl.ds(r, GROUP)
        x = product(k_ref[0, at], v_ref[0, at])
        first = block * TILE + r
        kept = kept_rows(seg_ref, start, first) if slow else None
        for h in range(0, rows, 8):
            s = [state_ref[n, h:h + 8] for n in range(modes)]
            d = [decay_ref[n, h:h + 8] for n in range(modes)]
            for t in range(GROUP):
                xt = x[t, h:h + 8]
                if slow:
                    inside = first + t < count
                    s = [jnp.where(inside, s[n] * (d[n] * kept[t]) + xt, s[n]) for n in range(modes)]
                else:
                    s = [s[n] * d[n] + xt for n in range(modes)]
            for n in range(modes):
                state_ref[n, h:h + 8] = s[n]

    def step(g, carry):
        r = pl.multiple_of(g * GROUP, GROUP)
        begin = start + block * TILE + r
        before = seg_ref[jnp.maximum(begin - 1, 0)]
        after = seg_ref[jnp.minimum(begin + GROUP - 1, last)]
        is_slow = (before != after) | (block * TILE + r + GROUP > count)

        @pl.when(is_slow)
        def _():
            group(r, True)

        @pl.when(jnp.logical_not(is_slow))
        def _():
            group(r, False)

        return carry

    todo = jnp.clip((count - block * TILE + GROUP - 1) // GROUP, 0, TILE // GROUP)
    lax.fori_loop(0, todo, step, 0)


def greet(peers):
    barrier = pltpu.get_barrier_semaphore()
    for peer in peers:
        pl.semaphore_signal(barrier, inc=1, device_id=peer, device_id_type=MESH)
    pl.semaphore_wait(barrier, len(peers))


def around(axis, count, offset):
    return {axis: lax.rem(lax.axis_index(axis) + offset, count)}


def gather_kernel(groups, in_ref, streams_ref, out_ref, rows_ref, raw, laid, send_sem, recv_sem, in_sem, out_sem):
    me = lax.axis_index("ch")
    reads = [pltpu.make_async_copy(streams_ref.at[i], raw.at[i], in_sem.at[i]) for i in range(3)]
    writes = [pltpu.make_async_copy(laid.at[i], rows_ref.at[i], out_sem.at[i]) for i in range(3)]
    for read in reads:
        read.start()
    greet([around("ch", groups, off) for off in range(1, groups)])
    copies = []
    for off in sorted(range(1, groups), key=lambda o: abs(o - groups // 2)):
        copy = pltpu.make_async_remote_copy(
            src_ref=in_ref,
            dst_ref=out_ref.at[me],
            send_sem=send_sem.at[off],
            recv_sem=recv_sem.at[off],
            device_id=around("ch", groups, off),
            device_id_type=MESH,
        )
        copy.start()
        copies.append(copy)
    out_ref[me] = in_ref[...]
    capacity, width = raw.shape[1:]
    for i in range(3):
        reads[i].wait()

        def relay(g, carry, i=i):
            at = pl.ds(pl.multiple_of(g * 16, 16), 16)
            laid[i, at] = raw[i, at].astype(F32).reshape(16, width // LANES, LANES).astype(BF16)
            return carry

        lax.fori_loop(0, capacity // 16, relay, 0)
        writes[i].start()
    for copy in copies:
        copy.wait()
    for write in writes:
        write.wait()


def mix_kernel(groups, spans, modes, counts_ref, seg_ref, ends_ref, rate_ref, rows_ref, decay_ref, weight_ref, skip_ref, out_ref, got, ahead, reach, told, back, land, send_sem, recv_sem, state_ref, held, row_send, row_recv, own_sem, loaded_ref, load_sem):
    me = lax.axis_index("ch")
    load = pltpu.make_async_copy(rows_ref, loaded_ref, load_sem)
    load.start()
    span = lax.axis_index("ctx")
    others = [around("ch", groups, off) for off in range(1, groups)]
    elsewhere = [around("ctx", spans, off) for off in range(1, spans)]
    greet(others + elsewhere)

    def sent(src, dst, number, peer):
        copy = pltpu.make_async_remote_copy(
            src_ref=src,
            dst_ref=dst,
            send_sem=send_sem.at[number],
            recv_sem=recv_sem.at[number],
            device_id=peer,
            device_id_type=MESH,
        )
        copy.start()
        return copy

    copies = [sent(ends_ref.at[peer["ch"]], got.at[me], i, peer) for i, peer in enumerate(others)]
    got[me] = ends_ref[me]
    for copy in copies:
        copy.wait()
    length = seg_ref.shape[0]
    first_id, last_id = seg_ref[0], seg_ref[length - 1]
    rate = rate_ref[...]
    state = jnp.zeros(got.shape[1:], F32)
    passing = jnp.ones(got.shape[1:], F32)
    joins = []
    start, before = jnp.int32(0), first_id
    for j in range(groups):
        joins.append(jnp.where(seg_ref[jnp.clip(start, 0, length - 1)] == before, 1.0, 0.0).astype(F32))
        start = start + counts_ref[j]
        after = seg_ref[jnp.clip(start - 1, 0, length - 1)]
        through = jnp.where(before == after, 1.0, 0.0).astype(F32)
        factor = jnp.exp(rate * -counts_ref[j].astype(F32)) * through
        ahead[j] = state
        reach[j] = passing
        state = factor * state + got[j]
        passing = factor * passing
        before = after
    span_decay = jnp.exp(rate * -float(length))
    wide = (8, got.shape[2])
    row = lax.broadcasted_iota(jnp.int32, wide, 0)
    edges = jnp.where(row == 0, jnp.full(wide, first_id.astype(F32)), jnp.full(wide, last_id.astype(F32)))
    told[span, 0:modes] = state
    told[span, modes:modes + 8] = edges
    copies = [sent(told.at[span], told.at[span], groups + i, peer) for i, peer in enumerate(elsewhere)]
    for copy in copies:
        copy.wait()
    state_in = jnp.zeros(got.shape[1:], F32)
    arriving = jnp.zeros(got.shape[1:], F32)
    for i in range(spans):
        initial, last = told[i, modes:modes + 1], told[i, modes + 1:modes + 2]
        if i > 0:
            arriving = jnp.where(initial == told[i - 1, modes + 1:modes + 2], 1.0, 0.0) * arriving
        state_in = jnp.where(span == i, arriving, state_in)
        arriving = told[i, 0:modes] + jnp.where(initial == last, 1.0, 0.0) * span_decay * arriving
    for j in range(groups):
        back[j] = joins[j] * (ahead[j] + reach[j] * state_in)
    copies = [sent(back.at[peer["ch"]], land.at[me], groups + spans + i, peer) for i, peer in enumerate(others)]
    land[me] = back[me]
    for copy in copies:
        copy.wait()
    for g in range(groups):
        for h in range(2):
            state_ref[:, 2 * g + h, :] = land[g, :, h * LANES:(h + 1) * LANES]

    capacity, rows = loaded_ref.shape[1:3]
    start = own_rows(counts_ref, groups)
    load.wait()
    order = sorted(range(1, groups), key=lambda off: abs(off - groups // 2))

    def group(first):
        kept = kept_rows(seg_ref, start, first)
        at = pl.ds(first, GROUP)
        x = product(loaded_ref[1, at], loaded_ref[2, at])
        q = loaded_ref[0, at].astype(F32)
        parts = []
        for h in range(0, rows, 8):
            s = [state_ref[n, h:h + 8] for n in range(modes)]
            d = [decay_ref[n, h:h + 8] for n in range(modes)]
            w = [weight_ref[n, h:h + 8] for n in range(modes)]
            skip = skip_ref[h:h + 8]
            mixed = []
            for t in range(GROUP):
                xt = x[t, h:h + 8]
                s = [s[n] * (d[n] * kept[t]) + xt for n in range(modes)]
                terms = [s[n] * w[n] for n in range(modes)]
                while len(terms) > 1:
                    terms = [a + b for a, b in zip(terms[::2], terms[1::2])]
                mixed.append(q[t, h:h + 8] * (terms[0] + skip * xt))
            for n in range(modes):
                state_ref[n, h:h + 8] = s[n]
            parts.append(mixed)
        for t in range(GROUP):
            whole = jnp.concatenate([part[t] for part in parts], axis=0).astype(BF16)
            for g in range(groups):
                held[g, first + t] = whole[2 * g:2 * g + 2]

    def copy_of(off, at):
        peer = around("ch", groups, off)
        return pltpu.make_async_remote_copy(
            src_ref=held.at[peer["ch"], at],
            dst_ref=out_ref.at[me, at],
            send_sem=row_send.at[off],
            recv_sem=row_recv.at[off],
            device_id=peer,
            device_id_type=MESH,
        )

    def block(b, carry):
        def step(g, inner):
            group(b * PIECE + g * GROUP)
            return inner

        lax.fori_loop(0, PIECE // GROUP, step, 0)
        at = pl.ds(b * PIECE, PIECE)
        for off in order:
            copy_of(off, at).start()
        return carry

    lax.fori_loop(0, capacity // PIECE, block, 0)
    own = pltpu.make_async_copy(held.at[me], out_ref.at[me], own_sem)
    own.start()
    for off in range(1, groups):
        copy_of(off, pl.ds(0, capacity)).wait()
    own.wait()


def pack_kernel(counts_ref, in_ref, out_ref):
    def shard(j, start):
        count = counts_ref[j]
        even = (count // GROUP) * GROUP

        def step(i, inner):
            m = i * GROUP
            out_ref[pl.ds(start + m, GROUP)] = in_ref[j, pl.ds(m, GROUP)]
            return inner

        def single(m, inner):
            out_ref[pl.ds(start + m, 1)] = in_ref[j, pl.ds(m, 1)]
            return inner

        lax.fori_loop(0, count // GROUP, step, 0)
        lax.fori_loop(even, count, single, 0)
        return start + count

    lax.fori_loop(0, in_ref.shape[0], shard, jnp.int32(0))


def smem():
    return pl.BlockSpec(memory_space=pltpu.SMEM)


def shards(streams, load_counts, seg_ids, rates, residues, skip):
    capacity, _, width = streams.shape
    groups = lax.axis_size("ch")
    spans = lax.axis_size("ctx")
    channels, modes = rates.shape
    length = seg_ids.shape[0]
    rows = width // LANES
    sub = channels // LANES

    rate_rows = rates.T
    gain = jnp.sqrt(-jnp.expm1(-2.0 * rate_rows))
    packed = jnp.concatenate([jnp.exp(-rate_rows), residues.T * gain, skip[None]], axis=0)
    vmem = pl.BlockSpec(memory_space=pltpu.VMEM)
    anywhere = pl.BlockSpec(memory_space=pl.ANY)
    every, loaded = pl.pallas_call(
        functools.partial(gather_kernel, groups),
        out_shape=(
            jax.ShapeDtypeStruct((groups,) + packed.shape, F32),
            jax.ShapeDtypeStruct((3, capacity, rows, LANES), BF16),
        ),
        in_specs=[vmem, anywhere],
        out_specs=(vmem, anywhere),
        scratch_shapes=[
            pltpu.VMEM((3, capacity, width), BF16),
            pltpu.VMEM((3, capacity, rows, LANES), BF16),
            pltpu.SemaphoreType.DMA((groups,)),
            pltpu.SemaphoreType.DMA((groups,)),
            pltpu.SemaphoreType.DMA((3,)),
            pltpu.SemaphoreType.DMA((3,)),
        ],
        compiler_params=pltpu.CompilerParams(collective_id=0, has_side_effects=True, vmem_limit_bytes=ROOM),
    )(packed, jnp.transpose(streams, (1, 0, 2)))
    every = every.reshape(groups, 2 * modes + 1, sub, LANES).transpose(1, 0, 2, 3).reshape(2 * modes + 1, rows, LANES)
    decay, weight, skip_all = every[:modes], every[modes:2 * modes], every[2 * modes]

    counts = load_counts[0]
    steps = capacity // TILE
    stream_of = lambda i: pl.BlockSpec((1, TILE, rows, LANES), lambda b: (i, b, 0, 0))
    fixed = lambda *shape: pl.BlockSpec(shape, lambda b: (0,) * len(shape))
    local_end = pl.pallas_call(
        functools.partial(end_state_kernel, modes, groups),
        grid=(steps,),
        out_shape=jax.ShapeDtypeStruct((modes, rows, LANES), F32),
        in_specs=[smem(), smem(), stream_of(1), stream_of(2), fixed(modes, rows, LANES)],
        out_specs=fixed(modes, rows, LANES),
        compiler_params=pltpu.CompilerParams(vmem_limit_bytes=ROOM),
    )(counts, seg_ids, loaded, loaded, decay)

    outgoing = local_end.reshape(modes, groups, channels).transpose(1, 0, 2)

    flat = pltpu.VMEM((groups, modes, channels), F32)
    slots = 2 * groups + spans
    arrived = pl.pallas_call(
        functools.partial(mix_kernel, groups, spans, modes),
        out_shape=jax.ShapeDtypeStruct((groups, capacity, sub, LANES), BF16),
        in_specs=[smem(), smem(), vmem, vmem, anywhere, vmem, vmem, vmem],
        out_specs=vmem,
        scratch_shapes=[
            flat,
            flat,
            flat,
            pltpu.VMEM((spans, modes + 8, channels), F32),
            flat,
            flat,
            pltpu.SemaphoreType.DMA((slots,)),
            pltpu.SemaphoreType.DMA((slots,)),
            pltpu.VMEM((modes, rows, LANES), F32),
            pltpu.VMEM((groups, capacity, sub, LANES), BF16),
            pltpu.SemaphoreType.DMA((groups,)),
            pltpu.SemaphoreType.DMA((groups,)),
            pltpu.SemaphoreType.DMA,
            pltpu.VMEM((3, capacity, rows, LANES), BF16),
            pltpu.SemaphoreType.DMA,
        ],
        compiler_params=pltpu.CompilerParams(collective_id=1, has_side_effects=True, vmem_limit_bytes=ROOM),
    )(counts, seg_ids, outgoing, rate_rows, loaded, decay, weight, skip_all)

    placed = pl.pallas_call(
        pack_kernel,
        out_shape=jax.ShapeDtypeStruct((length, sub, LANES), BF16),
        in_specs=[smem(), vmem],
        out_specs=vmem,
        compiler_params=pltpu.CompilerParams(vmem_limit_bytes=16 << 20),
    )(counts, arrived)
    return placed.reshape(length, channels)


def solution(mesh):
    return jax.shard_map(
        shards,
        mesh=mesh,
        in_specs=(
            P(("ctx", "ch"), None, None),
            P("ctx", None),
            P("ctx"),
            P("ch", None),
            P("ch", None),
            P("ch"),
        ),
        out_specs=P("ctx", "ch"),
        check_vma=False,
    )
```

```python
import functools

import jax
import jax.numpy as jnp
from jax import lax
from jax.experimental import pallas as pl
from jax.experimental.pallas import tpu as pltpu
from jax.sharding import PartitionSpec as P

LANES = 128
GROUP = 8
TILE = 128
PIECE = 64
ROOM = 50 << 20
MESH = pl.DeviceIdType.MESH
F32 = jnp.float32
BF16 = jnp.bfloat16


def product(k, v):
    return (k.astype(F32) * v.astype(F32)).astype(BF16).astype(F32)


def own_rows(counts_ref, number):
    me = lax.axis_index("ch")
    start = jnp.int32(0)
    for j in range(number):
        start = start + jnp.where(j < me, counts_ref[j], 0)
    return start


def kept_rows(seg_ref, start, first):
    last = seg_ref.shape[0] - 1
    ids = [seg_ref[jnp.clip(start + first + t, 0, last)] for t in range(-1, GROUP)]
    kept = [jnp.where(a == b, 1.0, 0.0).astype(F32) for a, b in zip(ids, ids[1:])]
    kept[0] = jnp.where(first == 0, 1.0, kept[0])
    return kept


def end_state_kernel(modes, groups, counts_ref, seg_ref, k_ref, v_ref, decay_ref, state_ref):
    block = pl.program_id(0)
    rows = k_ref.shape[2]
    count = counts_ref[lax.axis_index("ch")]
    start = own_rows(counts_ref, groups)
    last = seg_ref.shape[0] - 1

    @pl.when(block == 0)
    def _():
        state_ref[...] = jnp.zeros_like(state_ref)

    def group(r, slow):
        at = pl.ds(r, GROUP)
        x = product(k_ref[0, at], v_ref[0, at])
        first = block * TILE + r
        kept = kept_rows(seg_ref, start, first) if slow else None
        for h in range(0, rows, 8):
            s = [state_ref[n, h:h + 8] for n in range(modes)]
            d = [decay_ref[n, h:h + 8] for n in range(modes)]
            for t in range(GROUP):
                xt = x[t, h:h + 8]
                if slow:
                    inside = first + t < count
                    s = [jnp.where(inside, s[n] * (d[n] * kept[t]) + xt, s[n]) for n in range(modes)]
                else:
                    s = [s[n] * d[n] + xt for n in range(modes)]
            for n in range(modes):
                state_ref[n, h:h + 8] = s[n]

    def step(g, carry):
        r = pl.multiple_of(g * GROUP, GROUP)
        begin = start + block * TILE + r
        before = seg_ref[jnp.maximum(begin - 1, 0)]
        after = seg_ref[jnp.minimum(begin + GROUP - 1, last)]
        is_slow = (before != after) | (block * TILE + r + GROUP > count)

        @pl.when(is_slow)
        def _():
            group(r, True)

        @pl.when(jnp.logical_not(is_slow))
        def _():
            group(r, False)

        return carry

    todo = jnp.clip((count - block * TILE + GROUP - 1) // GROUP, 0, TILE // GROUP)
    lax.fori_loop(0, todo, step, 0)


def greet(peers):
    barrier = pltpu.get_barrier_semaphore()
    for peer in peers:
        pl.semaphore_signal(barrier, inc=1, device_id=peer, device_id_type=MESH)
    pl.semaphore_wait(barrier, len(peers))


def around(axis, count, offset):
    return {axis: lax.rem(lax.axis_index(axis) + offset, count)}


def gather_kernel(groups, in_ref, streams_ref, out_ref, rows_ref, raw, laid, send_sem, recv_sem, in_sem, out_sem):
    me = lax.axis_index("ch")
    reads = [pltpu.make_async_copy(streams_ref.at[i], raw.at[i], in_sem.at[i]) for i in range(3)]
    writes = [pltpu.make_async_copy(laid.at[i], rows_ref.at[i], out_sem.at[i]) for i in range(3)]
    for read in reads:
        read.start()
    greet([around("ch", groups, off) for off in range(1, groups)])
    copies = []
    for off in sorted(range(1, groups), key=lambda o: abs(o - groups // 2)):
        copy = pltpu.make_async_remote_copy(
            src_ref=in_ref,
            dst_ref=out_ref.at[me],
            send_sem=send_sem.at[off],
            recv_sem=recv_sem.at[off],
            device_id=around("ch", groups, off),
            device_id_type=MESH,
        )
        copy.start()
        copies.append(copy)
    out_ref[me] = in_ref[...]
    capacity, width = raw.shape[1:]
    for i in range(3):
        reads[i].wait()

        def relay(g, carry, i=i):
            at = pl.ds(pl.multiple_of(g * 16, 16), 16)
            laid[i, at] = raw[i, at].astype(F32).reshape(16, width // LANES, LANES).astype(BF16)
            return carry

        lax.fori_loop(0, capacity // 16, relay, 0)
        writes[i].start()
    for copy in copies:
        copy.wait()
    for write in writes:
        write.wait()


def mix_kernel(groups, spans, modes, counts_ref, seg_ref, ends_ref, rate_ref, rows_ref, decay_ref, weight_ref, skip_ref, out_ref, got, ahead, reach, told, back, land, send_sem, recv_sem, state_ref, held, row_send, row_recv, own_sem, loaded_ref, load_sem):
    me = lax.axis_index("ch")
    load = pltpu.make_async_copy(rows_ref, loaded_ref, load_sem)
    load.start()
    span = lax.axis_index("ctx")
    others = [around("ch", groups, off) for off in range(1, groups)]
    elsewhere = [around("ctx", spans, off) for off in range(1, spans)]
    greet(others + elsewhere)

    def sent(src, dst, number, peer):
        copy = pltpu.make_async_remote_copy(
            src_ref=src,
            dst_ref=dst,
            send_sem=send_sem.at[number],
            recv_sem=recv_sem.at[number],
            device_id=peer,
            device_id_type=MESH,
        )
        copy.start()
        return copy

    copies = [sent(ends_ref.at[peer["ch"]], got.at[me], i, peer) for i, peer in enumerate(others)]
    got[me] = ends_ref[me]
    for copy in copies:
        copy.wait()
    length = seg_ref.shape[0]
    first_id, last_id = seg_ref[0], seg_ref[length - 1]
    rate = rate_ref[...]
    state = jnp.zeros(got.shape[1:], F32)
    passing = jnp.ones(got.shape[1:], F32)
    joins = []
    start, before = jnp.int32(0), first_id
    for j in range(groups):
        joins.append(jnp.where(seg_ref[jnp.clip(start, 0, length - 1)] == before, 1.0, 0.0).astype(F32))
        start = start + counts_ref[j]
        after = seg_ref[jnp.clip(start - 1, 0, length - 1)]
        through = jnp.where(before == after, 1.0, 0.0).astype(F32)
        factor = jnp.exp(rate * -counts_ref[j].astype(F32)) * through
        ahead[j] = state
        reach[j] = passing
        state = factor * state + got[j]
        passing = factor * passing
        before = after
    span_decay = jnp.exp(rate * -float(length))
    wide = (8, got.shape[2])
    row = lax.broadcasted_iota(jnp.int32, wide, 0)
    edges = jnp.where(row == 0, jnp.full(wide, first_id.astype(F32)), jnp.full(wide, last_id.astype(F32)))
    told[span, 0:modes] = state
    told[span, modes:modes + 8] = edges
    copies = [sent(told.at[span], told.at[span], groups + i, peer) for i, peer in enumerate(elsewhere)]
    for copy in copies:
        copy.wait()
    state_in = jnp.zeros(got.shape[1:], F32)
    arriving = jnp.zeros(got.shape[1:], F32)
    for i in range(spans):
        initial, last = told[i, modes:modes + 1], told[i, modes + 1:modes + 2]
        if i > 0:
            arriving = jnp.where(initial == told[i - 1, modes + 1:modes + 2], 1.0, 0.0) * arriving
        state_in = jnp.where(span == i, arriving, state_in)
        arriving = told[i, 0:modes] + jnp.where(initial == last, 1.0, 0.0) * span_decay * arriving
    for j in range(groups):
        back[j] = joins[j] * (ahead[j] + reach[j] * state_in)
    copies = [sent(back.at[peer["ch"]], land.at[me], groups + spans + i, peer) for i, peer in enumerate(others)]
    land[me] = back[me]
    for copy in copies:
        copy.wait()
    for g in range(groups):
        for h in range(2):
            state_ref[:, 2 * g + h, :] = land[g, :, h * LANES:(h + 1) * LANES]

    capacity, rows = loaded_ref.shape[1:3]
    start = own_rows(counts_ref, groups)
    load.wait()
    order = sorted(range(1, groups), key=lambda off: abs(off - groups // 2))

    def group(first):
        kept = kept_rows(seg_ref, start, first)
        at = pl.ds(first, GROUP)
        x = product(loaded_ref[1, at], loaded_ref[2, at])
        q = loaded_ref[0, at].astype(F32)
        parts = []
        for h in range(0, rows, 8):
            s = [state_ref[n, h:h + 8] for n in range(modes)]
            d = [decay_ref[n, h:h + 8] for n in range(modes)]
            w = [weight_ref[n, h:h + 8] for n in range(modes)]
            skip = skip_ref[h:h + 8]
            mixed = []
            for t in range(GROUP):
                xt = x[t, h:h + 8]
                s = [s[n] * (d[n] * kept[t]) + xt for n in range(modes)]
                terms = [s[n] * w[n] for n in range(modes)]
                while len(terms) > 1:
                    terms = [a + b for a, b in zip(terms[::2], terms[1::2])]
                mixed.append(q[t, h:h + 8] * (terms[0] + skip * xt))
            for n in range(modes):
                state_ref[n, h:h + 8] = s[n]
            parts.append(mixed)
        for t in range(GROUP):
            whole = jnp.concatenate([part[t] for part in parts], axis=0).astype(BF16)
            for g in range(groups):
                held[g, first + t] = whole[2 * g:2 * g + 2]

    def copy_of(off, at):
        peer = around("ch", groups, off)
        return pltpu.make_async_remote_copy(
            src_ref=held.at[peer["ch"], at],
            dst_ref=out_ref.at[me, at],
            send_sem=row_send.at[off],
            recv_sem=row_recv.at[off],
            device_id=peer,
            device_id_type=MESH,
        )

    def block(b, carry):
        def step(g, inner):
            group(b * PIECE + g * GROUP)
            return inner

        lax.fori_loop(0, PIECE // GROUP, step, 0)
        at = pl.ds(b * PIECE, PIECE)
        for off in order:
            copy_of(off, at).start()
        return carry

    lax.fori_loop(0, capacity // PIECE, block, 0)
    own = pltpu.make_async_copy(held.at[me], out_ref.at[me], own_sem)
    own.start()
    for off in range(1, groups):
        copy_of(off, pl.ds(0, capacity)).wait()
    own.wait()


def pack_kernel(counts_ref, in_ref, out_ref):
    def shard(j, start):
        count = counts_ref[j]
        even = (count // GROUP) * GROUP

        def step(i, inner):
            m = i * GROUP
            out_ref[pl.ds(start + m, GROUP)] = in_ref[j, pl.ds(m, GROUP)]
            return inner

        def single(m, inner):
            out_ref[pl.ds(start + m, 1)] = in_ref[j, pl.ds(m, 1)]
            return inner

        lax.fori_loop(0, count // GROUP, step, 0)
        lax.fori_loop(even, count, single, 0)
        return start + count

    lax.fori_loop(0, in_ref.shape[0], shard, jnp.int32(0))


def smem():
    return pl.BlockSpec(memory_space=pltpu.SMEM)


def shards(streams, load_counts, seg_ids, rates, residues, skip):
    capacity, _, width = streams.shape
    groups = lax.axis_size("ch")
    spans = lax.axis_size("ctx")
    channels, modes = rates.shape
    length = seg_ids.shape[0]
    rows = width // LANES
    sub = channels // LANES

    rate_rows = rates.T
    gain = jnp.sqrt(-jnp.expm1(-2.0 * rate_rows))
    packed = jnp.concatenate([jnp.exp(-rate_rows), residues.T * gain, skip[None]], axis=0)
    vmem = pl.BlockSpec(memory_space=pltpu.VMEM)
    anywhere = pl.BlockSpec(memory_space=pl.ANY)
    every, loaded = pl.pallas_call(
        functools.partial(gather_kernel, groups),
        out_shape=(
            jax.ShapeDtypeStruct((groups,) + packed.shape, F32),
            jax.ShapeDtypeStruct((3, capacity, rows, LANES), BF16),
        ),
        in_specs=[vmem, anywhere],
        out_specs=(vmem, anywhere),
        scratch_shapes=[
            pltpu.VMEM((3, capacity, width), BF16),
            pltpu.VMEM((3, capacity, rows, LANES), BF16),
            pltpu.SemaphoreType.DMA((groups,)),
            pltpu.SemaphoreType.DMA((groups,)),
            pltpu.SemaphoreType.DMA((3,)),
            pltpu.SemaphoreType.DMA((3,)),
        ],
        compiler_params=pltpu.CompilerParams(collective_id=0, has_side_effects=True, vmem_limit_bytes=ROOM),
    )(packed, jnp.transpose(streams, (1, 0, 2)))
    every = every.reshape(groups, 2 * modes + 1, sub, LANES).transpose(1, 0, 2, 3).reshape(2 * modes + 1, rows, LANES)
    decay, weight, skip_all = every[:modes], every[modes:2 * modes], every[2 * modes]

    counts = load_counts[0]
    steps = capacity // TILE
    stream_of = lambda i: pl.BlockSpec((1, TILE, rows, LANES), lambda b: (i, b, 0, 0))
    fixed = lambda *shape: pl.BlockSpec(shape, lambda b: (0,) * len(shape))
    local_end = pl.pallas_call(
        functools.partial(end_state_kernel, modes, groups),
        grid=(steps,),
        out_shape=jax.ShapeDtypeStruct((modes, rows, LANES), F32),
        in_specs=[smem(), smem(), stream_of(1), stream_of(2), fixed(modes, rows, LANES)],
        out_specs=fixed(modes, rows, LANES),
        compiler_params=pltpu.CompilerParams(vmem_limit_bytes=ROOM),
    )(counts, seg_ids, loaded, loaded, decay)

    outgoing = local_end.reshape(modes, groups, channels).transpose(1, 0, 2)

    flat = pltpu.VMEM((groups, modes, channels), F32)
    slots = 2 * groups + spans
    arrived = pl.pallas_call(
        functools.partial(mix_kernel, groups, spans, modes),
        out_shape=jax.ShapeDtypeStruct((groups, capacity, sub, LANES), BF16),
        in_specs=[smem(), smem(), vmem, vmem, anywhere, vmem, vmem, vmem],
        out_specs=vmem,
        scratch_shapes=[
            flat,
            flat,
            flat,
            pltpu.VMEM((spans, modes + 8, channels), F32),
            flat,
            flat,
            pltpu.SemaphoreType.DMA((slots,)),
            pltpu.SemaphoreType.DMA((slots,)),
            pltpu.VMEM((modes, rows, LANES), F32),
            pltpu.VMEM((groups, capacity, sub, LANES), BF16),
            pltpu.SemaphoreType.DMA((groups,)),
            pltpu.SemaphoreType.DMA((groups,)),
            pltpu.SemaphoreType.DMA,
            pltpu.VMEM((3, capacity, rows, LANES), BF16),
            pltpu.SemaphoreType.DMA,
        ],
        compiler_params=pltpu.CompilerParams(collective_id=1, has_side_effects=True, vmem_limit_bytes=ROOM),
    )(counts, seg_ids, outgoing, rate_rows, loaded, decay, weight, skip_all)

    placed = pl.pallas_call(
        pack_kernel,
        out_shape=jax.ShapeDtypeStruct((length, sub, LANES), BF16),
        in_specs=[smem(), vmem],
        out_specs=vmem,
        compiler_params=pltpu.CompilerParams(vmem_limit_bytes=16 << 20),
    )(counts, arrived)
    return placed.reshape(length, channels)


def solution(mesh):
    return jax.shard_map(
        shards,
        mesh=mesh,
        in_specs=(
            P(("ctx", "ch"), None, None),
            P("ctx", None),
            P("ctx"),
            P("ch", None),
            P("ch", None),
            P("ch"),
        ),
        out_specs=P("ctx", "ch"),
        check_vma=False,
    )
```

```python
import functools

import jax
import jax.numpy as jnp
from jax import lax
from jax.experimental import pallas as pl
from jax.experimental.pallas import tpu as pltpu
from jax.sharding import PartitionSpec as P

LANES = 128
GROUP = 8
TILE = 128
PIECE = 16
ROOM = 50 << 20
MESH = pl.DeviceIdType.MESH
F32 = jnp.float32
BF16 = jnp.bfloat16


def product(k, v):
    return (k.astype(F32) * v.astype(F32)).astype(BF16).astype(F32)


def own_rows(counts_ref, number):
    me = lax.axis_index("ch")
    start = jnp.int32(0)
    for j in range(number):
        start = start + jnp.where(j < me, counts_ref[j], 0)
    return start


def kept_rows(seg_ref, start, first):
    last = seg_ref.shape[0] - 1
    ids = [seg_ref[jnp.clip(start + first + t, 0, last)] for t in range(-1, GROUP)]
    kept = [jnp.where(a == b, 1.0, 0.0).astype(F32) for a, b in zip(ids, ids[1:])]
    kept[0] = jnp.where(first == 0, 1.0, kept[0])
    return kept


def end_state_kernel(modes, groups, counts_ref, seg_ref, k_ref, v_ref, decay_ref, state_ref):
    block = pl.program_id(0)
    rows = k_ref.shape[2]
    count = counts_ref[lax.axis_index("ch")]
    start = own_rows(counts_ref, groups)
    last = seg_ref.shape[0] - 1

    @pl.when(block == 0)
    def _():
        state_ref[...] = jnp.zeros_like(state_ref)

    def group(r, slow):
        at = pl.ds(r, GROUP)
        x = product(k_ref[0, at], v_ref[0, at])
        first = block * TILE + r
        kept = kept_rows(seg_ref, start, first) if slow else None
        for h in range(0, rows, 8):
            s = [state_ref[n, h:h + 8] for n in range(modes)]
            d = [decay_ref[n, h:h + 8] for n in range(modes)]
            for t in range(GROUP):
                xt = x[t, h:h + 8]
                if slow:
                    inside = first + t < count
                    s = [jnp.where(inside, s[n] * (d[n] * kept[t]) + xt, s[n]) for n in range(modes)]
                else:
                    s = [s[n] * d[n] + xt for n in range(modes)]
            for n in range(modes):
                state_ref[n, h:h + 8] = s[n]

    def step(g, carry):
        r = pl.multiple_of(g * GROUP, GROUP)
        begin = start + block * TILE + r
        before = seg_ref[jnp.maximum(begin - 1, 0)]
        after = seg_ref[jnp.minimum(begin + GROUP - 1, last)]
        is_slow = (before != after) | (block * TILE + r + GROUP > count)

        @pl.when(is_slow)
        def _():
            group(r, True)

        @pl.when(jnp.logical_not(is_slow))
        def _():
            group(r, False)

        return carry

    todo = jnp.clip((count - block * TILE + GROUP - 1) // GROUP, 0, TILE // GROUP)
    lax.fori_loop(0, todo, step, 0)


def greet(peers):
    barrier = pltpu.get_barrier_semaphore()
    for peer in peers:
        pl.semaphore_signal(barrier, inc=1, device_id=peer, device_id_type=MESH)
    pl.semaphore_wait(barrier, len(peers))


def around(axis, count, offset):
    return {axis: lax.rem(lax.axis_index(axis) + offset, count)}


def gather_kernel(groups, in_ref, streams_ref, out_ref, rows_ref, raw, laid, send_sem, recv_sem, in_sem, out_sem):
    me = lax.axis_index("ch")
    reads = [pltpu.make_async_copy(streams_ref.at[i], raw.at[i], in_sem.at[i]) for i in range(3)]
    writes = [pltpu.make_async_copy(laid.at[i], rows_ref.at[i], out_sem.at[i]) for i in range(3)]
    for read in reads:
        read.start()
    greet([around("ch", groups, off) for off in range(1, groups)])
    copies = []
    for off in sorted(range(1, groups), key=lambda o: abs(o - groups // 2)):
        copy = pltpu.make_async_remote_copy(
            src_ref=in_ref,
            dst_ref=out_ref.at[me],
            send_sem=send_sem.at[off],
            recv_sem=recv_sem.at[off],
            device_id=around("ch", groups, off),
            device_id_type=MESH,
        )
        copy.start()
        copies.append(copy)
    out_ref[me] = in_ref[...]
    capacity, width = raw.shape[1:]
    for i in range(3):
        reads[i].wait()

        def relay(g, carry, i=i):
            at = pl.ds(pl.multiple_of(g * 16, 16), 16)
            laid[i, at] = raw[i, at].astype(F32).reshape(16, width // LANES, LANES).astype(BF16)
            return carry

        lax.fori_loop(0, capacity // 16, relay, 0)
        writes[i].start()
    for copy in copies:
        copy.wait()
    for write in writes:
        write.wait()


def mix_kernel(groups, spans, modes, counts_ref, seg_ref, ends_ref, rate_ref, rows_ref, decay_ref, weight_ref, skip_ref, out_ref, got, ahead, reach, told, back, land, send_sem, recv_sem, state_ref, held, row_send, row_recv, own_sem, loaded_ref, load_sem):
    me = lax.axis_index("ch")
    load = pltpu.make_async_copy(rows_ref, loaded_ref, load_sem)
    load.start()
    span = lax.axis_index("ctx")
    others = [around("ch", groups, off) for off in range(1, groups)]
    elsewhere = [around("ctx", spans, off) for off in range(1, spans)]
    greet(others + elsewhere)

    def sent(src, dst, number, peer):
        copy = pltpu.make_async_remote_copy(
            src_ref=src,
            dst_ref=dst,
            send_sem=send_sem.at[number],
            recv_sem=recv_sem.at[number],
            device_id=peer,
            device_id_type=MESH,
        )
        copy.start()
        return copy

    copies = [sent(ends_ref.at[peer["ch"]], got.at[me], i, peer) for i, peer in enumerate(others)]
    got[me] = ends_ref[me]
    for copy in copies:
        copy.wait()
    length = seg_ref.shape[0]
    first_id, last_id = seg_ref[0], seg_ref[length - 1]
    rate = rate_ref[...]
    state = jnp.zeros(got.shape[1:], F32)
    passing = jnp.ones(got.shape[1:], F32)
    joins = []
    start, before = jnp.int32(0), first_id
    for j in range(groups):
        joins.append(jnp.where(seg_ref[jnp.clip(start, 0, length - 1)] == before, 1.0, 0.0).astype(F32))
        start = start + counts_ref[j]
        after = seg_ref[jnp.clip(start - 1, 0, length - 1)]
        through = jnp.where(before == after, 1.0, 0.0).astype(F32)
        factor = jnp.exp(rate * -counts_ref[j].astype(F32)) * through
        ahead[j] = state
        reach[j] = passing
        state = factor * state + got[j]
        passing = factor * passing
        before = after
    span_decay = jnp.exp(rate * -float(length))
    wide = (8, got.shape[2])
    row = lax.broadcasted_iota(jnp.int32, wide, 0)
    edges = jnp.where(row == 0, jnp.full(wide, first_id.astype(F32)), jnp.full(wide, last_id.astype(F32)))
    told[span, 0:modes] = state
    told[span, modes:modes + 8] = edges
    copies = [sent(told.at[span], told.at[span], groups + i, peer) for i, peer in enumerate(elsewhere)]
    for copy in copies:
        copy.wait()
    state_in = jnp.zeros(got.shape[1:], F32)
    arriving = jnp.zeros(got.shape[1:], F32)
    for i in range(spans):
        initial, last = told[i, modes:modes + 1], told[i, modes + 1:modes + 2]
        if i > 0:
            arriving = jnp.where(initial == told[i - 1, modes + 1:modes + 2], 1.0, 0.0) * arriving
        state_in = jnp.where(span == i, arriving, state_in)
        arriving = told[i, 0:modes] + jnp.where(initial == last, 1.0, 0.0) * span_decay * arriving
    for j in range(groups):
        back[j] = joins[j] * (ahead[j] + reach[j] * state_in)
    copies = [sent(back.at[peer["ch"]], land.at[me], groups + spans + i, peer) for i, peer in enumerate(others)]
    land[me] = back[me]
    for copy in copies:
        copy.wait()
    for g in range(groups):
        for h in range(2):
            state_ref[:, 2 * g + h, :] = land[g, :, h * LANES:(h + 1) * LANES]

    capacity, rows = loaded_ref.shape[1:3]
    start = own_rows(counts_ref, groups)
    load.wait()
    order = sorted(range(1, groups), key=lambda off: abs(off - groups // 2))

    def group(first):
        kept = kept_rows(seg_ref, start, first)
        at = pl.ds(first, GROUP)
        x = product(loaded_ref[1, at], loaded_ref[2, at])
        q = loaded_ref[0, at].astype(F32)
        parts = []
        for h in range(0, rows, 8):
            s = [state_ref[n, h:h + 8] for n in range(modes)]
            d = [decay_ref[n, h:h + 8] for n in range(modes)]
            w = [weight_ref[n, h:h + 8] for n in range(modes)]
            skip = skip_ref[h:h + 8]
            mixed = []
            for t in range(GROUP):
                xt = x[t, h:h + 8]
                s = [s[n] * (d[n] * kept[t]) + xt for n in range(modes)]
                terms = [s[n] * w[n] for n in range(modes)]
                while len(terms) > 1:
                    terms = [a + b for a, b in zip(terms[::2], terms[1::2])]
                mixed.append(q[t, h:h + 8] * (terms[0] + skip * xt))
            for n in range(modes):
                state_ref[n, h:h + 8] = s[n]
            parts.append(mixed)
        for t in range(GROUP):
            whole = jnp.concatenate([part[t] for part in parts], axis=0).astype(BF16)
            for g in range(groups):
                held[g, first + t] = whole[2 * g:2 * g + 2]

    def copy_of(off, at):
        peer = around("ch", groups, off)
        return pltpu.make_async_remote_copy(
            src_ref=held.at[peer["ch"], at],
            dst_ref=out_ref.at[me, at],
            send_sem=row_send.at[off],
            recv_sem=row_recv.at[off],
            device_id=peer,
            device_id_type=MESH,
        )

    def block(b, carry):
        def step(g, inner):
            group(b * PIECE + g * GROUP)
            return inner

        lax.fori_loop(0, PIECE // GROUP, step, 0)
        at = pl.ds(b * PIECE, PIECE)
        for off in order:
            copy_of(off, at).start()
        return carry

    lax.fori_loop(0, capacity // PIECE, block, 0)
    own = pltpu.make_async_copy(held.at[me], out_ref.at[me], own_sem)
    own.start()
    for off in range(1, groups):
        copy_of(off, pl.ds(0, capacity)).wait()
    own.wait()


def pack_kernel(counts_ref, in_ref, out_ref):
    def shard(j, start):
        count = counts_ref[j]
        even = (count // GROUP) * GROUP

        def step(i, inner):
            m = i * GROUP
            out_ref[pl.ds(start + m, GROUP)] = in_ref[j, pl.ds(m, GROUP)]
            return inner

        def single(m, inner):
            out_ref[pl.ds(start + m, 1)] = in_ref[j, pl.ds(m, 1)]
            return inner

        lax.fori_loop(0, count // GROUP, step, 0)
        lax.fori_loop(even, count, single, 0)
        return start + count

    lax.fori_loop(0, in_ref.shape[0], shard, jnp.int32(0))


def smem():
    return pl.BlockSpec(memory_space=pltpu.SMEM)


def shards(streams, load_counts, seg_ids, rates, residues, skip):
    capacity, _, width = streams.shape
    groups = lax.axis_size("ch")
    spans = lax.axis_size("ctx")
    channels, modes = rates.shape
    length = seg_ids.shape[0]
    rows = width // LANES
    sub = channels // LANES

    rate_rows = rates.T
    gain = jnp.sqrt(-jnp.expm1(-2.0 * rate_rows))
    packed = jnp.concatenate([jnp.exp(-rate_rows), residues.T * gain, skip[None]], axis=0)
    vmem = pl.BlockSpec(memory_space=pltpu.VMEM)
    anywhere = pl.BlockSpec(memory_space=pl.ANY)
    every, loaded = pl.pallas_call(
        functools.partial(gather_kernel, groups),
        out_shape=(
            jax.ShapeDtypeStruct((groups,) + packed.shape, F32),
            jax.ShapeDtypeStruct((3, capacity, rows, LANES), BF16),
        ),
        in_specs=[vmem, anywhere],
        out_specs=(vmem, anywhere),
        scratch_shapes=[
            pltpu.VMEM((3, capacity, width), BF16),
            pltpu.VMEM((3, capacity, rows, LANES), BF16),
            pltpu.SemaphoreType.DMA((groups,)),
            pltpu.SemaphoreType.DMA((groups,)),
            pltpu.SemaphoreType.DMA((3,)),
            pltpu.SemaphoreType.DMA((3,)),
        ],
        compiler_params=pltpu.CompilerParams(collective_id=0, has_side_effects=True, vmem_limit_bytes=ROOM),
    )(packed, jnp.transpose(streams, (1, 0, 2)))
    every = every.reshape(groups, 2 * modes + 1, sub, LANES).transpose(1, 0, 2, 3).reshape(2 * modes + 1, rows, LANES)
    decay, weight, skip_all = every[:modes], every[modes:2 * modes], every[2 * modes]

    counts = load_counts[0]
    steps = capacity // TILE
    stream_of = lambda i: pl.BlockSpec((1, TILE, rows, LANES), lambda b: (i, b, 0, 0))
    fixed = lambda *shape: pl.BlockSpec(shape, lambda b: (0,) * len(shape))
    local_end = pl.pallas_call(
        functools.partial(end_state_kernel, modes, groups),
        grid=(steps,),
        out_shape=jax.ShapeDtypeStruct((modes, rows, LANES), F32),
        in_specs=[smem(), smem(), stream_of(1), stream_of(2), fixed(modes, rows, LANES)],
        out_specs=fixed(modes, rows, LANES),
        compiler_params=pltpu.CompilerParams(vmem_limit_bytes=ROOM),
    )(counts, seg_ids, loaded, loaded, decay)

    outgoing = local_end.reshape(modes, groups, channels).transpose(1, 0, 2)

    flat = pltpu.VMEM((groups, modes, channels), F32)
    slots = 2 * groups + spans
    arrived = pl.pallas_call(
        functools.partial(mix_kernel, groups, spans, modes),
        out_shape=jax.ShapeDtypeStruct((groups, capacity, sub, LANES), BF16),
        in_specs=[smem(), smem(), vmem, vmem, anywhere, vmem, vmem, vmem],
        out_specs=vmem,
        scratch_shapes=[
            flat,
            flat,
            flat,
            pltpu.VMEM((spans, modes + 8, channels), F32),
            flat,
            flat,
            pltpu.SemaphoreType.DMA((slots,)),
            pltpu.SemaphoreType.DMA((slots,)),
            pltpu.VMEM((modes, rows, LANES), F32),
            pltpu.VMEM((groups, capacity, sub, LANES), BF16),
            pltpu.SemaphoreType.DMA((groups,)),
            pltpu.SemaphoreType.DMA((groups,)),
            pltpu.SemaphoreType.DMA,
            pltpu.VMEM((3, capacity, rows, LANES), BF16),
            pltpu.SemaphoreType.DMA,
        ],
        compiler_params=pltpu.CompilerParams(collective_id=1, has_side_effects=True, vmem_limit_bytes=ROOM),
    )(counts, seg_ids, outgoing, rate_rows, loaded, decay, weight, skip_all)

    placed = pl.pallas_call(
        pack_kernel,
        out_shape=jax.ShapeDtypeStruct((length, sub, LANES), BF16),
        in_specs=[smem(), vmem],
        out_specs=vmem,
        compiler_params=pltpu.CompilerParams(vmem_limit_bytes=16 << 20),
    )(counts, arrived)
    return placed.reshape(length, channels)


def solution(mesh):
    return jax.shard_map(
        shards,
        mesh=mesh,
        in_specs=(
            P(("ctx", "ch"), None, None),
            P("ctx", None),
            P("ctx"),
            P("ch", None),
            P("ch", None),
            P("ch"),
        ),
        out_specs=P("ctx", "ch"),
        check_vma=False,
    )
```

```python
import functools

import jax
import jax.numpy as jnp
from jax import lax
from jax.experimental import pallas as pl
from jax.experimental.pallas import tpu as pltpu
from jax.sharding import PartitionSpec as P

LANES = 128
GROUP = 8
TILE = 128
PIECE = 16
ROOM = 50 << 20
MESH = pl.DeviceIdType.MESH
F32 = jnp.float32
BF16 = jnp.bfloat16


def product(k, v):
    return (k.astype(F32) * v.astype(F32)).astype(BF16).astype(F32)


def own_rows(counts_ref, number):
    me = lax.axis_index("ch")
    start = jnp.int32(0)
    for j in range(number):
        start = start + jnp.where(j < me, counts_ref[j], 0)
    return start


def kept_rows(seg_ref, start, first):
    last = seg_ref.shape[0] - 1
    ids = [seg_ref[jnp.clip(start + first + t, 0, last)] for t in range(-1, GROUP)]
    kept = [jnp.where(a == b, 1.0, 0.0).astype(F32) for a, b in zip(ids, ids[1:])]
    kept[0] = jnp.where(first == 0, 1.0, kept[0])
    return kept


def end_state_kernel(modes, groups, counts_ref, seg_ref, k_ref, v_ref, decay_ref, state_ref):
    block = pl.program_id(0)
    rows = k_ref.shape[2]
    count = counts_ref[lax.axis_index("ch")]
    start = own_rows(counts_ref, groups)
    last = seg_ref.shape[0] - 1

    @pl.when(block == 0)
    def _():
        state_ref[...] = jnp.zeros_like(state_ref)

    def group(r, slow):
        at = pl.ds(r, GROUP)
        x = product(k_ref[0, at], v_ref[0, at])
        first = block * TILE + r
        kept = kept_rows(seg_ref, start, first) if slow else None
        for h in range(0, rows, 8):
            s = [state_ref[n, h:h + 8] for n in range(modes)]
            d = [decay_ref[n, h:h + 8] for n in range(modes)]
            for t in range(GROUP):
                xt = x[t, h:h + 8]
                if slow:
                    inside = first + t < count
                    s = [jnp.where(inside, s[n] * (d[n] * kept[t]) + xt, s[n]) for n in range(modes)]
                else:
                    s = [s[n] * d[n] + xt for n in range(modes)]
            for n in range(modes):
                state_ref[n, h:h + 8] = s[n]

    def step(g, carry):
        r = pl.multiple_of(g * GROUP, GROUP)
        begin = start + block * TILE + r
        before = seg_ref[jnp.maximum(begin - 1, 0)]
        after = seg_ref[jnp.minimum(begin + GROUP - 1, last)]
        is_slow = (before != after) | (block * TILE + r + GROUP > count)

        @pl.when(is_slow)
        def _():
            group(r, True)

        @pl.when(jnp.logical_not(is_slow))
        def _():
            group(r, False)

        return carry

    todo = jnp.clip((count - block * TILE + GROUP - 1) // GROUP, 0, TILE // GROUP)
    lax.fori_loop(0, todo, step, 0)


def greet(peers):
    barrier = pltpu.get_barrier_semaphore()
    for peer in peers:
        pl.semaphore_signal(barrier, inc=1, device_id=peer, device_id_type=MESH)
    pl.semaphore_wait(barrier, len(peers))


def around(axis, count, offset):
    return {axis: lax.rem(lax.axis_index(axis) + offset, count)}


def gather_kernel(groups, in_ref, streams_ref, out_ref, rows_ref, raw, laid, send_sem, recv_sem, in_sem, out_sem):
    me = lax.axis_index("ch")
    reads = [pltpu.make_async_copy(streams_ref.at[i], raw.at[i], in_sem.at[i]) for i in range(3)]
    writes = [pltpu.make_async_copy(laid.at[i], rows_ref.at[i], out_sem.at[i]) for i in range(3)]
    for read in reads:
        read.start()
    greet([around("ch", groups, off) for off in range(1, groups)])
    copies = []
    for off in sorted(range(1, groups), key=lambda o: abs(o - groups // 2)):
        copy = pltpu.make_async_remote_copy(
            src_ref=in_ref,
            dst_ref=out_ref.at[me],
            send_sem=send_sem.at[off],
            recv_sem=recv_sem.at[off],
            device_id=around("ch", groups, off),
            device_id_type=MESH,
        )
        copy.start()
        copies.append(copy)
    out_ref[me] = in_ref[...]
    capacity, width = raw.shape[1:]
    for i in range(3):
        reads[i].wait()

        def relay(g, carry, i=i):
            at = pl.ds(pl.multiple_of(g * 16, 16), 16)
            laid[i, at] = raw[i, at].astype(F32).reshape(16, width // LANES, LANES).astype(BF16)
            return carry

        lax.fori_loop(0, capacity // 16, relay, 0)
        writes[i].start()
    for copy in copies:
        copy.wait()
    for write in writes:
        write.wait()


def mix_kernel(groups, spans, modes, counts_ref, seg_ref, ends_ref, rate_ref, rows_ref, decay_ref, weight_ref, skip_ref, out_ref, got, ahead, reach, told, back, land, send_sem, recv_sem, state_ref, held, row_send, row_recv, own_sem, loaded_ref, load_sem):
    me = lax.axis_index("ch")
    load = pltpu.make_async_copy(rows_ref, loaded_ref, load_sem)
    load.start()
    span = lax.axis_index("ctx")
    order = sorted(range(1, groups), key=lambda off: abs(off - groups // 2))
    others = [around("ch", groups, off) for off in order]
    sends = []
    elsewhere = [around("ctx", spans, off) for off in range(1, spans)]
    greet(others + elsewhere)

    def sent(src, dst, number, peer):
        copy = pltpu.make_async_remote_copy(
            src_ref=src,
            dst_ref=dst,
            send_sem=send_sem.at[number],
            recv_sem=recv_sem.at[number],
            device_id=peer,
            device_id_type=MESH,
        )
        copy.start()
        sends.append(copy)
        return copy

    copies = [sent(ends_ref.at[peer["ch"]], got.at[me], i, peer) for i, peer in enumerate(others)]
    got[me] = ends_ref[me]
    for copy in copies:
        copy.wait_recv()
    length = seg_ref.shape[0]
    first_id, last_id = seg_ref[0], seg_ref[length - 1]
    rate = rate_ref[...]
    state = jnp.zeros(got.shape[1:], F32)
    passing = jnp.ones(got.shape[1:], F32)
    joins = []
    start, before = jnp.int32(0), first_id
    for j in range(groups):
        joins.append(jnp.where(seg_ref[jnp.clip(start, 0, length - 1)] == before, 1.0, 0.0).astype(F32))
        start = start + counts_ref[j]
        after = seg_ref[jnp.clip(start - 1, 0, length - 1)]
        through = jnp.where(before == after, 1.0, 0.0).astype(F32)
        factor = jnp.exp(rate * -counts_ref[j].astype(F32)) * through
        ahead[j] = state
        reach[j] = passing
        state = factor * state + got[j]
        passing = factor * passing
        before = after
    span_decay = jnp.exp(rate * -float(length))
    wide = (8, got.shape[2])
    row = lax.broadcasted_iota(jnp.int32, wide, 0)
    edges = jnp.where(row == 0, jnp.full(wide, first_id.astype(F32)), jnp.full(wide, last_id.astype(F32)))
    told[span, 0:modes] = state
    told[span, modes:modes + 8] = edges
    copies = [sent(told.at[span], told.at[span], groups + i, peer) for i, peer in enumerate(elsewhere)]
    for copy in copies:
        copy.wait_recv()
    state_in = jnp.zeros(got.shape[1:], F32)
    arriving = jnp.zeros(got.shape[1:], F32)
    for i in range(spans):
        initial, last = told[i, modes:modes + 1], told[i, modes + 1:modes + 2]
        if i > 0:
            arriving = jnp.where(initial == told[i - 1, modes + 1:modes + 2], 1.0, 0.0) * arriving
        state_in = jnp.where(span == i, arriving, state_in)
        arriving = told[i, 0:modes] + jnp.where(initial == last, 1.0, 0.0) * span_decay * arriving
    for j in range(groups):
        back[j] = joins[j] * (ahead[j] + reach[j] * state_in)
    copies = [sent(back.at[peer["ch"]], land.at[me], groups + spans + i, peer) for i, peer in enumerate(others)]
    land[me] = back[me]
    for copy in copies:
        copy.wait_recv()
    for g in range(groups):
        for h in range(2):
            state_ref[:, 2 * g + h, :] = land[g, :, h * LANES:(h + 1) * LANES]

    capacity, rows = loaded_ref.shape[1:3]
    start = own_rows(counts_ref, groups)
    load.wait()

    def group(first):
        kept = kept_rows(seg_ref, start, first)
        at = pl.ds(first, GROUP)
        x = product(loaded_ref[1, at], loaded_ref[2, at])
        q = loaded_ref[0, at].astype(F32)
        parts = []
        for h in range(0, rows, 8):
            s = [state_ref[n, h:h + 8] for n in range(modes)]
            d = [decay_ref[n, h:h + 8] for n in range(modes)]
            w = [weight_ref[n, h:h + 8] for n in range(modes)]
            skip = skip_ref[h:h + 8]
            mixed = []
            for t in range(GROUP):
                xt = x[t, h:h + 8]
                s = [s[n] * (d[n] * kept[t]) + xt for n in range(modes)]
                terms = [s[n] * w[n] for n in range(modes)]
                while len(terms) > 1:
                    terms = [a + b for a, b in zip(terms[::2], terms[1::2])]
                mixed.append(q[t, h:h + 8] * (terms[0] + skip * xt))
            for n in range(modes):
                state_ref[n, h:h + 8] = s[n]
            parts.append(mixed)
        for t in range(GROUP):
            whole = jnp.concatenate([part[t] for part in parts], axis=0).astype(BF16)
            for g in range(groups):
                held[g, first + t] = whole[2 * g:2 * g + 2]

    def copy_of(off, at):
        peer = around("ch", groups, off)
        return pltpu.make_async_remote_copy(
            src_ref=held.at[peer["ch"], at],
            dst_ref=out_ref.at[me, at],
            send_sem=row_send.at[off],
            recv_sem=row_recv.at[off],
            device_id=peer,
            device_id_type=MESH,
        )

    def block(b, carry):
        def step(g, inner):
            group(b * PIECE + g * GROUP)
            return inner

        lax.fori_loop(0, PIECE // GROUP, step, 0)
        at = pl.ds(b * PIECE, PIECE)
        for off in order:
            copy_of(off, at).start()
        return carry

    lax.fori_loop(0, capacity // PIECE, block, 0)
    own = pltpu.make_async_copy(held.at[me], out_ref.at[me], own_sem)
    own.start()
    for off in range(1, groups):
        copy_of(off, pl.ds(0, capacity)).wait()
    own.wait()
    for send in sends:
        send.wait_send()


def pack_kernel(counts_ref, in_ref, out_ref):
    def shard(j, start):
        count = counts_ref[j]
        even = (count // GROUP) * GROUP

        def step(i, inner):
            m = i * GROUP
            out_ref[pl.ds(start + m, GROUP)] = in_ref[j, pl.ds(m, GROUP)]
            return inner

        def single(m, inner):
            out_ref[pl.ds(start + m, 1)] = in_ref[j, pl.ds(m, 1)]
            return inner

        lax.fori_loop(0, count // GROUP, step, 0)
        lax.fori_loop(even, count, single, 0)
        return start + count

    lax.fori_loop(0, in_ref.shape[0], shard, jnp.int32(0))


def smem():
    return pl.BlockSpec(memory_space=pltpu.SMEM)


def shards(streams, load_counts, seg_ids, rates, residues, skip):
    capacity, _, width = streams.shape
    groups = lax.axis_size("ch")
    spans = lax.axis_size("ctx")
    channels, modes = rates.shape
    length = seg_ids.shape[0]
    rows = width // LANES
    sub = channels // LANES

    rate_rows = rates.T
    gain = jnp.sqrt(-jnp.expm1(-2.0 * rate_rows))
    packed = jnp.concatenate([jnp.exp(-rate_rows), residues.T * gain, skip[None]], axis=0)
    vmem = pl.BlockSpec(memory_space=pltpu.VMEM)
    anywhere = pl.BlockSpec(memory_space=pl.ANY)
    every, loaded = pl.pallas_call(
        functools.partial(gather_kernel, groups),
        out_shape=(
            jax.ShapeDtypeStruct((groups,) + packed.shape, F32),
            jax.ShapeDtypeStruct((3, capacity, rows, LANES), BF16),
        ),
        in_specs=[vmem, anywhere],
        out_specs=(vmem, anywhere),
        scratch_shapes=[
            pltpu.VMEM((3, capacity, width), BF16),
            pltpu.VMEM((3, capacity, rows, LANES), BF16),
            pltpu.SemaphoreType.DMA((groups,)),
            pltpu.SemaphoreType.DMA((groups,)),
            pltpu.SemaphoreType.DMA((3,)),
            pltpu.SemaphoreType.DMA((3,)),
        ],
        compiler_params=pltpu.CompilerParams(collective_id=0, has_side_effects=True, vmem_limit_bytes=ROOM),
    )(packed, jnp.transpose(streams, (1, 0, 2)))
    every = every.reshape(groups, 2 * modes + 1, sub, LANES).transpose(1, 0, 2, 3).reshape(2 * modes + 1, rows, LANES)
    decay, weight, skip_all = every[:modes], every[modes:2 * modes], every[2 * modes]

    counts = load_counts[0]
    steps = capacity // TILE
    stream_of = lambda i: pl.BlockSpec((1, TILE, rows, LANES), lambda b: (i, b, 0, 0))
    fixed = lambda *shape: pl.BlockSpec(shape, lambda b: (0,) * len(shape))
    local_end = pl.pallas_call(
        functools.partial(end_state_kernel, modes, groups),
        grid=(steps,),
        out_shape=jax.ShapeDtypeStruct((modes, rows, LANES), F32),
        in_specs=[smem(), smem(), stream_of(1), stream_of(2), fixed(modes, rows, LANES)],
        out_specs=fixed(modes, rows, LANES),
        compiler_params=pltpu.CompilerParams(vmem_limit_bytes=ROOM),
    )(counts, seg_ids, loaded, loaded, decay)

    outgoing = local_end.reshape(modes, groups, channels).transpose(1, 0, 2)

    flat = pltpu.VMEM((groups, modes, channels), F32)
    slots = 2 * groups + spans
    arrived = pl.pallas_call(
        functools.partial(mix_kernel, groups, spans, modes),
        out_shape=jax.ShapeDtypeStruct((groups, capacity, sub, LANES), BF16),
        in_specs=[smem(), smem(), vmem, vmem, anywhere, vmem, vmem, vmem],
        out_specs=vmem,
        scratch_shapes=[
            flat,
            flat,
            flat,
            pltpu.VMEM((spans, modes + 8, channels), F32),
            flat,
            flat,
            pltpu.SemaphoreType.DMA((slots,)),
            pltpu.SemaphoreType.DMA((slots,)),
            pltpu.VMEM((modes, rows, LANES), F32),
            pltpu.VMEM((groups, capacity, sub, LANES), BF16),
            pltpu.SemaphoreType.DMA((groups,)),
            pltpu.SemaphoreType.DMA((groups,)),
            pltpu.SemaphoreType.DMA,
            pltpu.VMEM((3, capacity, rows, LANES), BF16),
            pltpu.SemaphoreType.DMA,
        ],
        compiler_params=pltpu.CompilerParams(collective_id=1, has_side_effects=True, vmem_limit_bytes=ROOM),
    )(counts, seg_ids, outgoing, rate_rows, loaded, decay, weight, skip_all)

    placed = pl.pallas_call(
        pack_kernel,
        out_shape=jax.ShapeDtypeStruct((length, sub, LANES), BF16),
        in_specs=[smem(), vmem],
        out_specs=vmem,
        compiler_params=pltpu.CompilerParams(vmem_limit_bytes=16 << 20),
    )(counts, arrived)
    return placed.reshape(length, channels)


def solution(mesh):
    return jax.shard_map(
        shards,
        mesh=mesh,
        in_specs=(
            P(("ctx", "ch"), None, None),
            P("ctx", None),
            P("ctx"),
            P("ch", None),
            P("ch", None),
            P("ch"),
        ),
        out_specs=P("ctx", "ch"),
        check_vma=False,
    )
```
